256 devices in a mesh: seq: 32 (over z, x), tp: 8 (over y, core).
Axes of the slice: x: 4, y: 4, z: 8, core: 2. Of those that a mesh axis runs over, the one named last changes fastest.
Arguments:
- queries: bfloat16 [8192, 4096], P('seq', 'tp'), may hold values from -6 to 6
- keys: bfloat16 [8192, 4096], P('seq', 'tp'), may hold values from -6 to 6
- values: bfloat16 [8192, 4096], P('seq', 'tp'), may hold values from -6 to 6
- log_decay: float32 [32, 8192], P('tp', 'seq'), may hold values from -1 to 0
- residual: bfloat16 [8192, 3072], P('seq', 'tp'), may hold values from -8 to 8
- out_weight: bfloat16 [4096, 3072], P('tp'), may hold values from -0.125 to 0.125
- prenorm_multiplier: float32 [3072], P('tp'), may hold values from 0.25 to 1.75
- router_weight: bfloat16 [3072, 32], replicated, may hold values from -0.109375 to 0.109375
- picked_unit_indices: int32 [8192, 2], P('seq'), may hold values from 0 to 31, all different within a row; in each aligned block of 256 rows (0 to 255, 256 to 511, ...) at most 24 rows name the same one
- expert_up_weight: bfloat16 [32, 3072, 5120], P('seq', None, 'tp'), may hold values from -0.109375 to 0.109375
- down_weight: bfloat16 [32, 5120, 3072], P('seq', 'tp'), may hold values from -0.125 to 0.125
Outputs:
- mixed: bfloat16 [8192, 3072], P('seq', 'tp')
The draws below stay inside these ranges and needn't reach their ends.
Inputs may be any that keep to these rules, and one draw needn't show every extreme that they name: `picked_unit_indices`: each row names 2 different experts. Among the rows of one slab of 256 positions no expert is named by more than 24 rows, and in every draw some expert is named by exactly 24 rows of some slab.
All inputs are finite; a program needn't handle non-finite values.
Results may differ from the reference program's by a relative error of at most 0.006.
Values may be sent and summed in bfloat16 or wider, within the bound.
A program may use at most 64 MiB of HBM per device.

```python
import math
import jax
import jax.numpy as jnp
import numpy as np
from jax import lax

D = 3072
ATTENTION_COUNT = 32
HEAD_DIM = 128
FF = 5120
TOP = 2
SLAB_POSITIONS = 256
TOKENS = 8192
EXPERTS = 32
CAP = 24
N_SEQ = 32
N_TP = 8


def draw_log_decay(key, part):
    key = jax.random.fold_in(key, 11)
    divided_random_seeds = jax.random.split(key, 7)
    fast_share = 0.5
    fast = jax.random.uniform(divided_random_seeds[0], (ATTENTION_COUNT,)) < fast_share
    fast_rate = jnp.exp(jax.random.uniform(divided_random_seeds[1], (ATTENTION_COUNT,), jnp.float32, math.log(1.0 / 50.0), math.log(1.0 / 30.0)))
    slow_rate = jnp.exp(jax.random.uniform(divided_random_seeds[2], (ATTENTION_COUNT,), jnp.float32, math.log(0.2), math.log(0.5))) / TOKENS
    default_shrink_speed = jnp.where(fast, fast_rate, slow_rate)
    segment_shrink_multiplier = jnp.exp(jax.random.uniform(divided_random_seeds[3], (ATTENTION_COUNT, TOKENS // SLAB_POSITIONS), jnp.float32, math.log(0.5), math.log(2.0)))
    segment_shrink_multiplier = jnp.repeat(segment_shrink_multiplier, SLAB_POSITIONS, axis=1)
    offset_shrink_multiplier = jnp.exp(jax.random.uniform(divided_random_seeds[4], (ATTENTION_COUNT, TOKENS), jnp.float32, math.log(0.5), math.log(2.0)))
    spots = jax.random.randint(divided_random_seeds[5], (ATTENTION_COUNT, 3), 0, TOKENS)
    load_imbalance_terms = jax.random.uniform(divided_random_seeds[6], (ATTENTION_COUNT, 3), jnp.float32, math.log(0.6), math.log(0.8))
    per_unit_token_counts = jnp.arange(TOKENS)[None, :, None] == spots[:, None, :]
    overload_instance_count = jnp.sum(jnp.where(per_unit_token_counts, load_imbalance_terms[:, None, :], 0.0), axis=2)
    return -default_shrink_speed[:, None] * segment_shrink_multiplier * offset_shrink_multiplier + overload_instance_count


def draw_residual(key, part):
    key = jax.random.fold_in(key, 23)
    divided_random_seeds = jax.random.split(key, 3)
    column_place = jnp.arange(D, dtype=jnp.float32)[None, :] / (D - 1)
    core = jax.random.normal(divided_random_seeds[0], (TOKENS, D))
    row_scale = jnp.exp(jax.random.uniform(divided_random_seeds[1], (TOKENS, 1), jnp.float32, math.log(0.3), math.log(3.0)))
    column_ramp = jnp.exp(math.log(0.3) + column_place * (math.log(3.0) - math.log(0.3)))
    column_scale = column_ramp * jnp.exp(jax.random.uniform(divided_random_seeds[2], (1, D), jnp.float32, math.log(0.7), math.log(1.4)))
    return jnp.clip(core * row_scale * column_scale, -8.0, 8.0).astype(jnp.bfloat16)


def spiked(array, own_key, source, target, shards_of, factor):
    def block_of(dim):
        return (jnp.arange(array.shape[dim]) // (array.shape[dim] // shards_of)).reshape((-1,) + (1,) * (array.ndim - 1 - dim))

    near = jax.random.permutation(own_key, shards_of)[block_of(target)]
    other_side = (block_of(target) + shards_of // 2) % shards_of
    return jnp.where((block_of(source) == near) | (block_of(source) == other_side), factor * array, array)


def level_of(stream_key, dims, pieces, low, top_value):
    gain, own = 1.0, jax.random.fold_in(stream_key, 6)
    for axis_at, parts in pieces:
        steps = jnp.exp(jax.random.uniform(jax.random.fold_in(own, axis_at), (parts,), jnp.float32, low / len(pieces), top_value / len(pieces)))
        gain = gain * jnp.repeat(steps, dims[axis_at] // parts).reshape([-1 if axis == axis_at else 1 for axis in range(len(dims))])
    return gain


def shared_out(key, own, number, rows, amount, top, most, lean):
    ranking = jax.random.permutation(key, amount)
    crowded, usual = load_shares(amount, rows * top, most, lean, True), load_shares(amount, rows * top, most, lean, False)
    places = jnp.arange(amount)

    def named(sizes, rotation):
        used = int((sizes > 0).sum())
        fixed = max(1, used // 4)
        shifted = fixed + (places - fixed + rotation * (used - fixed)) % max(1, amount - fixed)
        return jnp.zeros((amount,), jnp.int32).at[ranking[jnp.where(places < fixed, places, shifted)]].set(jnp.asarray(sizes, jnp.int32))

    sizes = jnp.where(number % 4 == 0, named(crowded, number // 4), named(usual, number - number // 4 - 1))
    mixed = jax.random.permutation(jax.random.fold_in(own, 3), amount)
    giver, receiver = mixed[0:amount // 2 * 2:2], mixed[1:amount // 2 * 2:2]
    slack = jnp.minimum(sizes[giver] - 1, most - sizes[receiver]) // 2
    slack = jnp.where((giver == ranking[0]) | (receiver == ranking[0]) | (sizes[receiver] == 0), 0, jnp.maximum(slack, 0))
    shifted = jax.random.randint(jax.random.fold_in(own, 4), (amount // 2,), 0, 1 << 20) % (slack + 1)
    sizes = sizes.at[giver].add(-shifted).at[receiver].add(shifted)
    members = jnp.searchsorted(jnp.cumsum(sizes), jnp.arange(rows * top), side="right").astype(jnp.int32)
    grid = members.reshape(top, rows).T
    grid = grid[jax.random.permutation(jax.random.fold_in(own, 1), rows)]
    rotation = jax.random.randint(jax.random.fold_in(own, 2), (rows, 1), 0, top)
    return jnp.take_along_axis(grid, (jnp.arange(top)[None, :] + rotation) % top, axis=1)


def load_shares(amount, total, reach, slope, full):
    loads = [(1 << 20) // math.isqrt(standing ** slope) + 1 for standing in range(1, amount + 1)]
    largest = reach if full else min(reach, max(-(-total // amount), total * loads[0] // sum(loads)))
    least = 1 if total - largest >= amount - 1 else 0
    counts, spare = [largest] + [least] * (amount - 1), total - largest - least * (amount - 1)
    while spare > 0:
        candidates = [i for i in range(1, amount) if counts[i] < largest] or [i for i in range(1, amount) if counts[i] < reach]
        mass, budget = sum([loads[i] for i in candidates]), spare
        for i in candidates:
            more = min(reach - counts[i], max(1, budget * loads[i] // mass), spare)
            counts[i] = counts[i] + more
            spare = spare - more
    return np.array(counts)


def gaussian(rng, extent, spread, reach, cuts=(), kind=jnp.bfloat16):
    values = spread * jax.random.normal(rng, extent, jnp.float32)
    if cuts:
        values = values * level_of(rng, extent, cuts, -0.22, 0.18)
    return jnp.clip(values, -reach, reach).astype(kind)


def heavy_noise(rng, dims, spread, bound, cuts, heavy, kind=jnp.bfloat16):
    entries = spread * jax.random.normal(rng, dims, jnp.float32)
    if cuts:
        entries = entries * level_of(rng, dims, cuts, -0.22, 0.18)
    return jnp.clip(spiked(entries, jax.random.fold_in(rng, 3), *heavy), -bound, bound).astype(kind)


def setup_inputs(seed: int = 0) -> dict:
    key_of = jax.random.split(jax.random.key(seed), 12)
    queries = gaussian(key_of[0], (TOKENS, ATTENTION_COUNT * HEAD_DIM), 1.0, 6.0, ((0, 32), (1, 8)))
    keys = gaussian(key_of[1], (TOKENS, ATTENTION_COUNT * HEAD_DIM), 1.0, 6.0, ((0, 32), (1, 8)))
    values = gaussian(key_of[2], (TOKENS, ATTENTION_COUNT * HEAD_DIM), 1.0, 6.0, ((0, 32), (1, 8)))
    log_decay = draw_log_decay(jax.random.fold_in(key_of[11], 71), 0)
    residual = draw_residual(jax.random.fold_in(key_of[11], 71), 0)
    out_weight = heavy_noise(key_of[5], (ATTENTION_COUNT * HEAD_DIM, D), (ATTENTION_COUNT * HEAD_DIM) ** -0.5, 0.125, ((0, 8),), (0, 1, 8, 2.0))
    prenorm_multiplier = jnp.clip(1.0 + 0.15 * jax.random.normal(key_of[6], (D,), jnp.float32), 0.25, 1.75)
    router_weight = gaussian(key_of[7], (D, EXPERTS), D ** -0.5, 0.109375)
    picked_unit_indices_keys = jax.random.split(jax.random.fold_in(key_of[8], 1), TOKENS // SLAB_POSITIONS)
    picked_unit_indices_turns = jax.random.permutation(jax.random.fold_in(key_of[8], 3), TOKENS // SLAB_POSITIONS)
    picked_unit_indices = jax.vmap(lambda own, number: shared_out(jax.random.fold_in(key_of[8], 2), own, number, SLAB_POSITIONS, EXPERTS, TOP, CAP, 1))(picked_unit_indices_keys, picked_unit_indices_turns).reshape((TOKENS, TOP))
    expert_up_weight = gaussian(key_of[9], (EXPERTS, D, FF), D ** -0.5, 0.109375, ((0, 32), (2, 8)))
    down_weight = heavy_noise(key_of[10], (EXPERTS, FF, D), FF ** -0.5, 0.125, ((0, 32), (1, 8)), (1, 2, 8, 2.0))
    return dict(queries=queries, keys=keys, values=values, log_decay=log_decay, residual=residual, out_weight=out_weight, prenorm_multiplier=prenorm_multiplier, router_weight=router_weight, picked_unit_indices=picked_unit_indices, expert_up_weight=expert_up_weight, down_weight=down_weight)


EPSILON = 1e-05

def head_norm(head_values):
    return head_values * lax.rsqrt(lax.optimization_barrier(jnp.mean(head_values * head_values, axis=-1, keepdims=True)) + EPSILON)

def slab_step(carried_state, inputs):
    query_heads, key_heads, value_heads, decay_logs = inputs
    cumulative = jnp.cumsum(decay_logs, axis=1)
    position = jnp.arange(decay_logs.shape[1], dtype=jnp.int32)
    causal = (position[:, None] >= position[None, :])[None]
    log_gap = jnp.where(causal, cumulative[:, :, None] - cumulative[:, None, :], 0.0)
    decay_matrix = jnp.where(causal, jnp.exp(log_gap), 0.0)
    scores = jnp.einsum('thd,shd->hts', query_heads, key_heads)
    intra_weights = (scores * decay_matrix).astype(jnp.bfloat16)
    within_slab = jnp.einsum('hts,she->the', intra_weights.astype(jnp.float32), value_heads)
    from_state = jnp.einsum('thd,hde->the', query_heads, carried_state, precision=lax.Precision.HIGHEST)
    head_out = within_slab + from_state * jnp.exp(cumulative).T[:, :, None]
    slab_total = cumulative[:, -1]
    weighted_keys = key_heads * jnp.exp(slab_total[None, :] - cumulative.T)[:, :, None]
    updated_memory_matrix = jnp.einsum('thd,the->hde', weighted_keys, value_heads, precision=lax.Precision.HIGHEST)
    next_memory_matrix = jnp.exp(slab_total)[:, None, None] * carried_state + updated_memory_matrix
    attended = head_norm(head_out).astype(jnp.bfloat16)
    return (next_memory_matrix, attended.reshape(attended.shape[0], -1))

def apply_specialist(inputs):
    row_block, up_matrix, down_matrix = inputs
    expert_hidden = jax.nn.silu(jnp.dot(row_block, up_matrix, preferred_element_type=jnp.float32)).astype(jnp.bfloat16)
    groups = expert_hidden.reshape(row_block.shape[0], N_TP, FF // N_TP).astype(jnp.float32)
    down_groups = down_matrix.reshape(N_TP, FF // N_TP, D).astype(jnp.float32)
    partial_value = jnp.einsum('rgf,gfd->grd', groups, down_groups).astype(jnp.bfloat16)
    partial_value = lax.optimization_barrier(partial_value)
    return lax.optimization_barrier(jnp.sum(partial_value.astype(jnp.float32), axis=0))

def reference(queries, keys, values, log_decay, residual, out_weight, prenorm_multiplier, router_weight, picked_unit_indices, expert_up_weight, down_weight):
    shaped = (N_SEQ, SLAB_POSITIONS, ATTENTION_COUNT, HEAD_DIM)
    slabs = (queries.astype(jnp.float32).reshape(shaped), keys.astype(jnp.float32).reshape(shaped), values.astype(jnp.float32).reshape(shaped), log_decay.reshape(ATTENTION_COUNT, N_SEQ, SLAB_POSITIONS).transpose(1, 0, 2))
    start_state = jnp.zeros((ATTENTION_COUNT, HEAD_DIM, HEAD_DIM), jnp.float32)
    _, attended = lax.scan(slab_step, start_state, slabs)
    attention = attended.reshape(TOKENS, ATTENTION_COUNT * HEAD_DIM)
    hidden_state = residual.astype(jnp.float32) + jnp.dot(attention, out_weight, preferred_element_type=jnp.float32)
    inverse_rms = lax.rsqrt(lax.optimization_barrier(jnp.mean(hidden_state * hidden_state, axis=1, keepdims=True)) + EPSILON)
    normed = (hidden_state * inverse_rms * prenorm_multiplier).astype(jnp.bfloat16)
    gate_values = jax.nn.sigmoid(jnp.dot(normed, router_weight, preferred_element_type=jnp.float32))
    picked_mask = picked_unit_indices[:, :, None] == jnp.arange(EXPERTS, dtype=jnp.int32)[None, None, :]
    chosen = lax.optimization_barrier(jnp.sum(jnp.where(picked_mask, gate_values[:, None, :], 0.0), axis=2))
    shares = chosen / lax.optimization_barrier(jnp.sum(chosen, axis=1, keepdims=True))
    flat_ids = picked_unit_indices.reshape(N_SEQ, TOP * SLAB_POSITIONS)
    onehot = (flat_ids[:, :, None] == jnp.arange(EXPERTS, dtype=jnp.int32)[None, None, :]).astype(jnp.int32)
    slot_index = lax.optimization_barrier(jnp.sum((jnp.cumsum(onehot, axis=1) - onehot) * onehot, axis=2))
    source = jnp.arange(N_SEQ, dtype=jnp.int32)[:, None]
    target = (flat_ids * (N_SEQ * CAP) + source * CAP + slot_index).reshape(-1).astype(jnp.int32)
    dispatch = jnp.zeros((EXPERTS * N_SEQ * CAP, D), jnp.bfloat16).at[target].set(jnp.repeat(normed, TOP, axis=0))
    expert_out = lax.map(apply_specialist, (dispatch.reshape(EXPERTS, N_SEQ * CAP, D), expert_up_weight, down_weight))
    picked = expert_out.reshape(EXPERTS * N_SEQ * CAP, D)[target].reshape(TOKENS, TOP, D)
    expert_mix = lax.optimization_barrier(jnp.sum(shares[:, :, None] * picked, axis=1))
    return (hidden_state + expert_mix).astype(jnp.bfloat16)
```

```python
import functools

import jax
import jax.numpy as jnp
from jax import lax
from jax.experimental import pallas as pl
from jax.experimental.pallas import tpu as pltpu
from jax.sharding import PartitionSpec as P

EPSILON = 1e-05
MESH = pl.DeviceIdType.MESH
F32, BF16 = jnp.float32, jnp.bfloat16
HIGHEST = lax.Precision.HIGHEST
CAP = 24
PAD = 32
CORES = 2


def mm(a, b):
    return jnp.dot(a, b, preferred_element_type=F32)


def mm_nt(a, b):
    return lax.dot_general(a, b, (((1,), (1,)), ((), ())), preferred_element_type=F32)


def mm_tn(a, b):
    return lax.dot_general(a, b, (((0,), (0,)), ((), ())), preferred_element_type=F32)


def iota(shape, dim):
    return lax.broadcasted_iota(jnp.int32, shape, dim)


def flag(mask):
    return jnp.where(mask, 1.0, 0.0).astype(BF16)


def split2(x):
    high = x.astype(BF16)
    return high, (x - high.astype(F32)).astype(BF16)


def to_column(row):
    n = row.shape[1]
    eye = iota((n, n), 0) == iota((n, n), 1)
    return jnp.sum(jnp.where(eye, row, 0.0), axis=1, keepdims=True)


def to_row(column):
    n = column.shape[0]
    eye = iota((n, n), 0) == iota((n, n), 1)
    return jnp.sum(jnp.where(eye, column, 0.0), axis=0, keepdims=True)


def send(src, dst, send_sem, recv_sem, device):
    pltpu.make_async_remote_copy(
        src_ref=src,
        dst_ref=dst,
        send_sem=send_sem,
        recv_sem=recv_sem,
        device_id=device,
        device_id_type=MESH,
    ).start()


def wait(ref, sem):
    pltpu.make_async_copy(ref, ref, sem).wait()


def scratch_of(c):
    n, y, g, w, t, hd = c["n"], c["y"], c["g"], c["w"], c["t"], c["hd"]
    tp, slots, rows, padded, f = y * CORES, c["slots"], c["rows"], c["padded"], c["f"]
    dma = pltpu.SemaphoreType.DMA
    return dict(
        owv=pltpu.VMEM((tp, c["a"], w), BF16),
        rwv=pltpu.VMEM((w, n), BF16),
        upv=pltpu.VMEM((y, CORES * w, f), BF16),
        dnv=pltpu.VMEM((y, f, CORES * w), BF16),
        ub=pltpu.VMEM((n, hd, 128), BF16),
        ur=pltpu.VMEM((n, hd, 128), BF16),
        ts=pltpu.VMEM((c["heads"], 1, 128), F32),
        tr=pltpu.VMEM((n, 1, 128), F32),
        sb=pltpu.VMEM((n, hd, 128), BF16),
        se=pltpu.VMEM((n, hd, 128), BF16),
        within=pltpu.VMEM((t, c["a"]), F32),
        ps1=pltpu.VMEM((y, t, w), BF16),
        pr1=pltpu.VMEM((y, t, w), BF16),
        ps2=pltpu.VMEM((y, t, w), BF16),
        pr2=pltpu.VMEM((y, t, w), BF16),
        sqs=pltpu.VMEM((1, t), F32),
        sqr=pltpu.VMEM((tp, 1, t), F32),
        cs=pltpu.VMEM((2, 1, t), F32),
        cr=pltpu.VMEM((tp, 2, 1, t), F32),
        pm=pltpu.VMEM((n * PAD, t), BF16),
        q0=pltpu.VMEM((t, n * PAD), BF16),
        q1=pltpu.VMEM((t, n * PAD), BF16),
        dsp=pltpu.VMEM((n * PAD, w), BF16),
        xr=pltpu.VMEM((g, padded, w), BF16),
        xg=pltpu.VMEM((g, y, rows, CORES * w), BF16),
        mb=pltpu.VMEM((g, y, rows, w), F32),
        ps=pltpu.VMEM((g, y, rows, w), BF16),
        pr=pltpu.VMEM((g, y, rows, w), BF16),
        ys=pltpu.VMEM((g, y, rows, w), BF16),
        yr=pltpu.VMEM((g, y, rows, w), BF16),
        hs=pltpu.VMEM((g, padded, w), BF16),
        ret=pltpu.VMEM((n * PAD, w), BF16),
        w_ow=dma((tp,)),
        w_up=dma((y,)),
        w_dn=dma((y,)),
        w_rw=dma((1,)),
        m_s=dma((8,)),
        m_r=dma((8,)),
        p1_s=dma((y,)),
        p1_r=dma((y,)),
        p2_s=dma((y,)),
        p2_r=dma((y,)),
        x_s=dma((g,)),
        x_r=dma((g,)),
        a_s=dma((g, y)),
        a_r=dma((g, y)),
        b_s=dma((g, y)),
        b_r=dma((g, y)),
        c_s=dma((g, y)),
        c_r=dma((g, y)),
        d_s=dma((g, y)),
        d_r=dma((g, y)),
        h_s=dma((g,)),
    )


def kernel(c, names, *refs):
    (q, k, v, ld, res, mult, ids, idst, ow, rw, up, dn, out) = refs[:13]
    r = dict(zip(names, refs[13:]))
    n, xs, zs, ys_n, groups = c["n"], c["x"], c["z"], c["y"], c["groups"]
    heads, t, w, hd, tp_n = c["heads"], c["t"], c["w"], c["hd"], c["y"] * CORES
    rows, padded, slots = c["rows"], c["padded"], c["slots"]
    s, tp = lax.axis_index("seq"), lax.axis_index("tp")
    z, x = s // xs, lax.rem(s, xs)
    y, core = tp // CORES, lax.rem(tp, CORES)
    partner = (s, y * CORES + 1 - core)
    m_s, m_r = r["m_s"], r["m_r"]

    def seq_peers(body):
        def step(i, carry):
            body(lax.rem(s + i, n))
            return carry

        lax.fori_loop(1, n, step, 0)

    def tp_peers(body):
        def step(i, carry):
            body(lax.rem(tp + i, tp_n))
            return carry

        lax.fori_loop(1, tp_n, step, 0)

    barrier = pltpu.get_barrier_semaphore()
    seq_peers(
        lambda p: pl.semaphore_signal(barrier, inc=1, device_id=(p, tp), device_id_type=MESH)
    )
    tp_peers(lambda p: pl.semaphore_signal(barrier, inc=1, device_id=(s, p), device_id_type=MESH))

    weights = []
    for u in range(tp_n):
        weights.append(
            pltpu.make_async_copy(ow.at[:, pl.ds(u * w, w)], r["owv"].at[u], r["w_ow"].at[u])
        )
    weights.append(
        pltpu.make_async_copy(
            rw.at[pl.ds(pl.multiple_of(tp * w, w), w), :], r["rwv"], r["w_rw"].at[0]
        )
    )
    for i in range(ys_n):
        part = pl.ds(i * CORES * w, CORES * w)
        weights.append(
            pltpu.make_async_copy(up.at[0, part, :], r["upv"].at[i], r["w_up"].at[i])
        )
    for i in range(ys_n):
        part = pl.ds(i * CORES * w, CORES * w)
        weights.append(
            pltpu.make_async_copy(dn.at[0, :, part], r["dnv"].at[i], r["w_dn"].at[i])
        )
    for copy in weights:
        copy.start()

    logs = ld[...]
    upper = jnp.where(iota((t, t), 0) <= iota((t, t), 1), 1.0, 0.0)
    lower = jnp.where(iota((t, t), 0) >= iota((t, t), 1), 1.0, 0.0)
    c_row = jnp.dot(logs, upper, precision=HIGHEST, preferred_element_type=F32)
    c_col = lax.dot_general(
        lower, logs, (((1,), (1,)), ((), ())), precision=HIGHEST, preferred_element_type=F32
    )
    per_head = 128 // hd
    for h in range(heads):
        head = pl.ds(h * 128, 128)
        total = c_row[h : h + 1, t - 1 : t]
        r["ts"][h] = jnp.broadcast_to(total, (1, 128))
        weighted = k[:, head].astype(F32) * jnp.exp(total - c_col[:, h : h + 1])
        high, low = split2(weighted)
        product = (mm_tn(high, v[:, head]) + mm_tn(low, v[:, head])).astype(BF16)
        for i in range(per_head):
            r["ub"][h * per_head + i] = product[i * hd : (i + 1) * hd]

    pl.semaphore_wait(barrier, n - 1 + tp_n - 1)

    ub, ur, ts, tr, sb, se = (r[name] for name in ("ub", "ur", "ts", "tr", "sb", "se"))
    seq_peers(lambda p: send(ts.at[p // per_head], tr.at[s], m_s.at[0], m_r.at[0], (p, tp)))
    seq_peers(lambda p: send(ub.at[p], ur.at[s], m_s.at[1], m_r.at[1], (p, tp)))
    tr[s] = ts[s // per_head]
    ur[s] = ub[s]

    ids_c = ids[...]
    ids_r = idst[...]
    first, second = ids_c[:, 0:1], ids_c[:, 1:2]
    names_lane = iota((t, n), 1)
    before = flag(iota((t, t), 1) < iota((t, t), 0))
    counts = mm(before, flag((first == names_lane) | (second == names_lane)))
    for j, pick, q_ref in ((0, first, r["q0"]), (1, second, r["q1"])):
        slot = jnp.sum(jnp.where(pick == names_lane, counts, 0.0), axis=1, keepdims=True)
        target = pick.astype(F32) * PAD + slot
        q_ref[...] = flag(iota((t, n * PAD), 1).astype(F32) == target)
    first, second = ids_r[0:1, :], ids_r[1:2, :]
    names_sub = iota((n, t), 0)
    after = flag(iota((t, t), 0) < iota((t, t), 1))
    counts = mm(flag((first == names_sub) | (second == names_sub)), after)
    targets = []
    for pick in (first, second):
        slot = jnp.sum(jnp.where(pick == names_sub, counts, 0.0), axis=0, keepdims=True)
        targets.append(pick.astype(F32) * PAD + slot)
    place = iota((n * PAD, t), 0).astype(F32)
    r["pm"][...] = flag((place == targets[0]) | (place == targets[1]))

    causal = iota((t, t), 0) >= iota((t, t), 1)
    for h in range(heads):
        head = pl.ds(h * 128, 128)
        scores = mm_nt(q[:, head], k[:, head])
        gap = jnp.where(causal, c_col[:, h : h + 1] - c_row[h : h + 1, :], 0.0)
        intra = jnp.where(causal, scores * jnp.exp(gap), 0.0).astype(BF16)
        r["within"][:, head] = mm(intra, v[:, head])

    wait(tr.at[pl.ds(0, n - 1)], m_r.at[0])
    wait(ur.at[pl.ds(0, n - 1)], m_r.at[1])

    def scan(b, state):
        sb[b] = state.astype(BF16)
        return jnp.exp(tr[b]) * state + ur[b].astype(F32)

    lax.fori_loop(0, n, scan, jnp.zeros((hd, 128), F32))
    seq_peers(lambda p: send(sb.at[p], se.at[s], m_s.at[2], m_r.at[2], (p, tp)))
    se[s] = sb[s]
    wait(se.at[pl.ds(0, n - 1)], m_r.at[2])

    attended = []
    for h in range(heads):
        head = pl.ds(h * 128, 128)
        state = se[h * per_head : (h + 1) * per_head].reshape(128, 128)
        head_out = r["within"][:, head] + mm(q[:, head], state) * jnp.exp(c_col[:, h : h + 1])
        mean = jnp.mean(head_out * head_out, axis=1, keepdims=True)
        attended.append((head_out * lax.rsqrt(mean + EPSILON)).astype(BF16))
    attention = jnp.concatenate(attended, axis=1)

    ps1, pr1, ps2, pr2 = (r[name] for name in ("ps1", "pr1", "ps2", "pr2"))
    for copy in weights[: tp_n + 1]:
        copy.wait()
    order = [d for d in (2, 1, 3) if d < ys_n] + [0]
    for d in order:
        to = lax.rem(y + d, ys_n)
        ps1[to] = mm(attention, r["owv"][to * CORES + 1 - core]).astype(BF16)
        send(ps1.at[to], pr1.at[to], r["p1_s"].at[to], r["p1_r"].at[to], partner)
    hidden = res[...].astype(F32)
    for d in order:
        to = lax.rem(y + d, ys_n)
        mine = mm(attention, r["owv"][to * CORES + core])
        wait(pr1.at[to], r["p1_r"].at[to])
        mine = mine + pr1[to].astype(F32)
        if d:
            ps2[d] = mine.astype(BF16)
            send(ps2.at[d], pr2.at[d], r["p2_s"].at[d], r["p2_r"].at[d], (s, to * CORES + core))
        else:
            hidden = hidden + mine
    for d in order[:-1]:
        wait(pr2.at[d], r["p2_r"].at[d])
        hidden = hidden + pr2[d].astype(F32)

    sqs, sqr = r["sqs"], r["sqr"]
    high, low = split2(hidden * hidden)
    ones = jnp.ones((8, w), BF16)
    sqs[...] = (mm_nt(ones, high) + mm_nt(ones, low))[0:1]
    tp_peers(lambda p: send(sqs, sqr.at[tp], m_s.at[3], m_r.at[3], (s, p)))
    sqr[tp] = sqs[...]
    wait(sqr.at[pl.ds(0, tp_n - 1)], m_r.at[3])
    square_sum = sqr[0]
    for u in range(1, tp_n):
        square_sum = square_sum + sqr[u]
    inverse = to_column(lax.rsqrt(square_sum / (w * tp_n) + EPSILON))
    normed = (hidden * inverse * mult[...]).astype(BF16)

    dsp, xr, ret = r["dsp"], r["xr"], r["ret"]
    dsp[...] = mm(r["pm"][...], normed).astype(BF16)

    def rows_of(index):
        return pl.ds(pl.multiple_of(index * PAD, PAD), PAD)

    def group_peers(g, sign, body):
        near, far = groups[g]

        def step(j, carry):
            dz = jnp.where(j < xs, near, far)
            dx = lax.rem(j, xs)
            pz = lax.rem(z + zs + sign * dz, zs)
            px = lax.rem(x + xs + sign * dx, xs)
            body(j, pz * xs + px)
            return carry

        lax.fori_loop(0 if near else 1, slots, step, 0)

    for g in range(len(groups)):
        group_peers(
            g,
            1,
            lambda j, p, g=g: send(
                dsp.at[rows_of(p)], xr.at[g, rows_of(j)], r["x_s"].at[g], r["x_r"].at[g], (p, tp)
            ),
        )
    last = len(groups) - 1
    xr[last, 0:PAD] = dsp[rows_of(s)]

    cs, cr = r["cs"], r["cr"]
    logits = mm(normed, r["rwv"][...])
    for j in range(2):
        chosen = jnp.where(ids_c[:, j : j + 1] == names_lane, logits, 0.0)
        cs[j] = to_row(jnp.sum(chosen, axis=1, keepdims=True))
    tp_peers(lambda p: send(cs, cr.at[tp], m_s.at[4], m_r.at[4], (s, p)))
    cr[tp] = cs[...]

    xg, mb, ps, pr, ys, yr, hs = (r[name] for name in ("xg", "mb", "ps", "pr", "ys", "yr", "hs"))
    compact_row, compact_lane = iota((rows, padded), 0), iota((rows, padded), 1)
    block = (compact_row * 2731) >> 16
    pack = flag(compact_lane == block * PAD + (compact_row - block * CAP))
    spread_row, spread_lane = iota((padded, rows), 0), iota((padded, rows), 1)
    block = (spread_lane * 2731) >> 16
    spread = flag(spread_row == block * PAD + (spread_lane - block * CAP))
    own_half = pl.ds(pl.multiple_of(core * w, w), w)
    other_half = pl.ds(pl.multiple_of((1 - core) * w, w), w)
    arrive = [d for d in (1, 3, 2) if d < ys_n]

    def spread_out(g):
        ref = xr.at[g] if groups[g][0] else xr.at[g, pl.ds(0, padded - PAD)]
        wait(ref, r["x_r"].at[g])
        packed = mm(pack, xr[g]).astype(BF16)
        for side in range(CORES):

            @pl.when(core == side)
            def _(side=side):
                xg[g, y, :, side * w : (side + 1) * w] = packed

        piece = xg.at[g, y, :, own_half]
        for d in order[:-1]:
            to = lax.rem(y + d, ys_n)
            send(piece, piece, r["a_s"].at[g, d], r["a_r"].at[g, d], (s, to * CORES + core))
        send(piece, piece, r["b_s"].at[g, 0], r["b_r"].at[g, 0], partner)

    def hand_over(g):
        for d in arrive:
            piece = xg.at[g, lax.rem(y + ys_n - d, ys_n), :, own_half]
            wait(piece, r["a_r"].at[g, d])
            send(piece, piece, r["b_s"].at[g, d], r["b_r"].at[g, d], partner)

    def expert(g):
        for d in range(ys_n):
            wait(
                xg.at[g, lax.rem(y + ys_n - d, ys_n), :, other_half],
                r["b_r"].at[g, d],
            )
        total = mm(xg[g, 0], r["upv"][0])
        for i in range(1, ys_n):
            total = total + mm(xg[g, i], r["upv"][i])
        hidden_rows = (total / (1.0 + jnp.exp(-total))).astype(BF16)
        for i in range(ys_n):
            part = mm(hidden_rows, r["dnv"][i])
            left, right = part[:, :w], part[:, w:]
            mb[g, i] = jnp.where(core == 0, left, right)
            ps[g, i] = jnp.where(core == 0, right, left).astype(BF16)
            send(ps.at[g, i], pr.at[g, i], r["c_s"].at[g, i], r["c_r"].at[g, i], partner)

    def over_y(g):
        for d in order[:-1]:
            to = lax.rem(y + d, ys_n)
            wait(pr.at[g, to], r["c_r"].at[g, to])
            ys[g, d] = (mb[g, to] + pr[g, to].astype(F32)).astype(BF16)
            send(
                ys.at[g, d],
                yr.at[g, d],
                r["d_s"].at[g, d],
                r["d_r"].at[g, d],
                (s, to * CORES + core),
            )

    def home(g):
        wait(pr.at[g, y], r["c_r"].at[g, y])
        total = mb[g, y] + pr[g, y].astype(F32)
        for d in arrive:
            wait(yr.at[g, d], r["d_r"].at[g, d])
            total = total + yr[g, d].astype(F32)
        hs[g] = mm(spread, total.astype(BF16)).astype(BF16)
        group_peers(
            g,
            -1,
            lambda j, p: send(
                hs.at[g, rows_of(j)], ret.at[rows_of(s)], r["h_s"].at[g], m_r.at[5], (p, tp)
            ),
        )
        if not groups[g][0]:
            ret[rows_of(s)] = hs[g, 0:PAD]

    for copy in weights[tp_n + 1 :]:
        copy.wait()
    stages = (spread_out, hand_over, expert, over_y, home)
    for step in range(len(groups) + len(stages) - 1):
        for lag, stage in enumerate(stages):
            if 0 <= step - lag < len(groups):
                stage(step - lag)

    wait(cr.at[pl.ds(0, tp_n - 1)], m_r.at[4])
    gates = []
    for j in range(2):
        logit = cr[0, j]
        for u in range(1, tp_n):
            logit = logit + cr[u, j]
        gates.append(jax.nn.sigmoid(logit))
    both = gates[0] + gates[1]
    shares = [to_column(gate / both) for gate in gates]
    wait(ret.at[pl.ds(0, (n - 1) * PAD)], m_r.at[5])
    returned = ret[...]
    mix = shares[0] * mm(r["q0"][...], returned) + shares[1] * mm(r["q1"][...], returned)
    out[...] = (hidden + mix).astype(BF16)

    wait(tr.at[pl.ds(0, n - 1)], m_s.at[0])
    wait(ur.at[pl.ds(0, n - 1)], m_s.at[1])
    wait(se.at[pl.ds(0, n - 1)], m_s.at[2])
    wait(sqr.at[pl.ds(0, tp_n - 1)], m_s.at[3])
    wait(cr.at[pl.ds(0, tp_n - 1)], m_s.at[4])
    for i in range(ys_n):
        wait(ps1.at[i], r["p1_s"].at[i])
    for d in order[:-1]:
        wait(ps2.at[d], r["p2_s"].at[d])
    for g in range(len(groups)):
        ref = xr.at[g] if groups[g][0] else xr.at[g, pl.ds(0, padded - PAD)]
        wait(ref, r["x_s"].at[g])
        wait(ref, r["h_s"].at[g])
        for d in range(ys_n):
            wait(ps.at[g, d], r["b_s"].at[g, d])
            wait(ps.at[g, d], r["c_s"].at[g, d])
            if d:
                wait(ps.at[g, d], r["a_s"].at[g, d])
                wait(ps.at[g, d], r["d_s"].at[g, d])


def body(
    sizes,
    queries,
    keys,
    values,
    log_decay,
    residual,
    out_weight,
    prenorm_multiplier,
    router_weight,
    picked_unit_indices,
    expert_up_weight,
    down_weight,
):
    n, xs, zs, ys = sizes
    half = zs // 2
    groups = [(d, zs - d) for d in range(1, half)] + [(0, half)]
    heads = log_decay.shape[0]
    slots = 2 * xs
    c = dict(
        n=n,
        x=xs,
        z=zs,
        y=ys,
        groups=groups,
        g=len(groups),
        heads=heads,
        t=queries.shape[0],
        a=queries.shape[1],
        w=residual.shape[1],
        f=expert_up_weight.shape[2],
        hd=heads * 128 // n,
        slots=slots,
        rows=slots * CAP,
        padded=slots * PAD,
    )
    scratch = scratch_of(c)
    vmem, anywhere = pl.BlockSpec(memory_space=pltpu.VMEM), pl.BlockSpec(memory_space=pl.ANY)
    return pl.pallas_call(
        functools.partial(kernel, c, list(scratch)),
        out_shape=jax.ShapeDtypeStruct(residual.shape, BF16),
        in_specs=[vmem] * 8 + [anywhere] * 4,
        out_specs=vmem,
        scratch_shapes=list(scratch.values()),
        compiler_params=pltpu.CompilerParams(
            collective_id=0, has_side_effects=True, vmem_limit_bytes=56 * 1024 * 1024
        ),
    )(
        queries,
        keys,
        values,
        log_decay,
        residual,
        prenorm_multiplier[None, :],
        picked_unit_indices,
        picked_unit_indices.T,
        out_weight,
        router_weight,
        expert_up_weight,
        down_weight,
    )


def solution(mesh):
    n = mesh.shape["seq"]
    xs = 4 if n % 4 == 0 and n > 4 else 2
    sizes = (n, xs, n // xs, mesh.shape["tp"] // CORES)
    in_specs = (
        P("seq", "tp"),
        P("seq", "tp"),
        P("seq", "tp"),
        P("tp", "seq"),
        P("seq", "tp"),
        P("tp", None),
        P("tp"),
        P(),
        P("seq", None),
        P("seq", None, "tp"),
        P("seq", "tp", None),
    )
    return jax.shard_map(
        functools.partial(body, sizes),
        mesh=mesh,
        in_specs=in_specs,
        out_specs=P("seq", "tp"),
        check_vma=False,
    )
```

```python
import functools

import jax
import jax.numpy as jnp
from jax import lax
from jax.experimental import pallas as pl
from jax.experimental.pallas import tpu as pltpu
from jax.sharding import PartitionSpec as P

EPSILON = 1e-05
MESH = pl.DeviceIdType.MESH
F32, BF16 = jnp.float32, jnp.bfloat16
HIGHEST = lax.Precision.HIGHEST
CAP = 24
PAD = 32
CORES = 2


def mm(a, b):
    return jnp.dot(a, b, preferred_element_type=F32)


def mm_nt(a, b):
    return lax.dot_general(a, b, (((1,), (1,)), ((), ())), preferred_element_type=F32)


def mm_tn(a, b):
    return lax.dot_general(a, b, (((0,), (0,)), ((), ())), preferred_element_type=F32)


def iota(shape, dim):
    return lax.broadcasted_iota(jnp.int32, shape, dim)


def flag(mask):
    return jnp.where(mask, 1.0, 0.0).astype(BF16)


def split2(x):
    high = x.astype(BF16)
    return high, (x - high.astype(F32)).astype(BF16)


def to_column(row):
    n = row.shape[1]
    eye = iota((n, n), 0) == iota((n, n), 1)
    return jnp.sum(jnp.where(eye, row, 0.0), axis=1, keepdims=True)


def to_row(column):
    n = column.shape[0]
    eye = iota((n, n), 0) == iota((n, n), 1)
    return jnp.sum(jnp.where(eye, column, 0.0), axis=0, keepdims=True)


def send(src, dst, send_sem, recv_sem, device):
    pltpu.make_async_remote_copy(
        src_ref=src,
        dst_ref=dst,
        send_sem=send_sem,
        recv_sem=recv_sem,
        device_id=device,
        device_id_type=MESH,
    ).start()


def wait(ref, sem):
    pltpu.make_async_copy(ref, ref, sem).wait()


def scratch_of(c):
    n, y, g, w, t, hd = c["n"], c["y"], c["g"], c["w"], c["t"], c["hd"]
    tp, f, rows = y * CORES, c["f"], n * CAP
    dma = pltpu.SemaphoreType.DMA
    return dict(
        owv=pltpu.VMEM((tp, c["a"], w), BF16),
        rwv=pltpu.VMEM((n, w), BF16),
        upv=pltpu.VMEM((y, CORES * w, f), BF16),
        dnv=pltpu.VMEM((y, f, CORES * w), BF16),
        ub=pltpu.VMEM((n, hd, 128), BF16),
        ur=pltpu.VMEM((n, hd, 128), BF16),
        ts=pltpu.VMEM((c["heads"], 1, 128), F32),
        tr=pltpu.VMEM((n, 1, 128), F32),
        sb=pltpu.VMEM((n, hd, 128), BF16),
        se=pltpu.VMEM((n, hd, 128), BF16),
        within=pltpu.VMEM((t, c["a"]), F32),
        ps1=pltpu.VMEM((y, t, w), BF16),
        pr1=pltpu.VMEM((y, t, w), BF16),
        ps2=pltpu.VMEM((y, t, w), BF16),
        pr2=pltpu.VMEM((y, t, w), BF16),
        rl1=pltpu.VMEM((2, t // 2, w), BF16),
        sqs=pltpu.VMEM((1, t), F32),
        sqr=pltpu.VMEM((tp, 1, t), F32),
        fs=pltpu.VMEM((n, 1, 128), F32),
        fr=pltpu.VMEM((n, 1, 128), F32),
        cs=pltpu.VMEM((2, 1, t), F32),
        cr=pltpu.VMEM((tp, 2, 1, t), F32),
        pm=pltpu.VMEM((n * PAD, t), BF16),
        q0=pltpu.VMEM((t, n * PAD), BF16),
        q1=pltpu.VMEM((t, n * PAD), BF16),
        dsp=pltpu.VMEM((n * PAD, w), BF16),
        xr=pltpu.VMEM((n * PAD, w), BF16),
        xg=pltpu.VMEM((y, rows, CORES * w), BF16),
        mb=pltpu.VMEM((y, rows, w), F32),
        ps=pltpu.VMEM((y, rows, w), BF16),
        pr=pltpu.VMEM((y, rows, w), BF16),
        ys=pltpu.VMEM((y, rows, w), BF16),
        yr=pltpu.VMEM((y, rows, w), BF16),
        rl=pltpu.VMEM((rows, w), BF16),
        hs=pltpu.VMEM((n * PAD, w), BF16),
        ret=pltpu.VMEM((n * PAD, w), BF16),
        w_ow=dma((tp,)),
        w_up=dma((y,)),
        w_dn=dma((y,)),
        w_rw=dma((1,)),
        m_s=dma((8,)),
        m_r=dma((8,)),
        p1_s=dma((y,)),
        p1_r=dma((y,)),
        p2_s=dma((y,)),
        p2_r=dma((y,)),
        p3_s=dma((2,)),
        p3_r=dma((2,)),
        l1_s=dma((2,)),
        l1_r=dma((2,)),
        x_s=dma((g,)),
        x_r=dma((g,)),
        a_s=dma((g, y)),
        a_r=dma((g, y)),
        b_s=dma((g, y)),
        b_r=dma((g, y)),
        c_s=dma((g, y)),
        c_r=dma((g, y)),
        d_s=dma((g, y)),
        d_r=dma((g, y)),
        e_s=dma((g, 2)),
        e_r=dma((g, 2)),
        f_s=dma((g, 2)),
        f_r=dma((g, 2)),
        l_s=dma((g, 2)),
        l_r=dma((g, 2)),
        h_s=dma((g,)),
    )


def kernel(c, names, *refs):
    (q, k, v, ld, res, mult, idst, ow, rw, up, dn, out) = refs[:12]
    r = dict(zip(names, refs[12:]))
    n, xs, zs, ys_n, groups = c["n"], c["x"], c["z"], c["y"], c["groups"]
    heads, t, w, hd, tp_n = c["heads"], c["t"], c["w"], c["hd"], c["y"] * CORES
    starts = [xs * sum(len(steps) for steps in groups[:g]) for g in range(len(groups))]
    sizes = [xs * len(steps) for steps in groups]
    s, tp = lax.axis_index("seq"), lax.axis_index("tp")
    z, x = s // xs, lax.rem(s, xs)
    y, core = tp // CORES, lax.rem(tp, CORES)
    partner = (s, y * CORES + 1 - core)
    ahead, behind, opposite = (lax.rem(y + d, ys_n) for d in (1, 3, 2))
    sides = ((ahead, (s, ahead * CORES + core)), (behind, (s, behind * CORES + core)))
    m_s, m_r = r["m_s"], r["m_r"]

    def seq_peers(body):
        def step(i, carry):
            distance = (n - i + 1) // 2
            body(lax.rem(s + jnp.where(lax.rem(i, 2) == 1, distance, n - distance), n))
            return carry

        lax.fori_loop(1, n, step, 0)

    def tp_peers(body):
        def step(i, carry):
            body(lax.rem(tp + i, tp_n))
            return carry

        lax.fori_loop(1, tp_n, step, 0)

    pending = []
    barrier = pltpu.get_barrier_semaphore()
    seq_peers(
        lambda p: pl.semaphore_signal(barrier, inc=1, device_id=(p, tp), device_id_type=MESH)
    )
    tp_peers(lambda p: pl.semaphore_signal(barrier, inc=1, device_id=(s, p), device_id_type=MESH))

    weights = []
    for u in range(tp_n):
        weights.append(
            pltpu.make_async_copy(ow.at[:, pl.ds(u * w, w)], r["owv"].at[u], r["w_ow"].at[u])
        )
    weights.append(
        pltpu.make_async_copy(
            rw.at[:, pl.ds(pl.multiple_of(tp * w, w), w)], r["rwv"], r["w_rw"].at[0]
        )
    )
    for i in range(ys_n):
        part = pl.ds(i * CORES * w, CORES * w)
        weights.append(
            pltpu.make_async_copy(up.at[0, part, :], r["upv"].at[i], r["w_up"].at[i])
        )
    for i in range(ys_n):
        part = pl.ds(i * CORES * w, CORES * w)
        weights.append(
            pltpu.make_async_copy(dn.at[0, :, part], r["dnv"].at[i], r["w_dn"].at[i])
        )
    for copy in weights:
        copy.start()

    logs = ld[...]
    upper = jnp.where(iota((t, t), 0) <= iota((t, t), 1), 1.0, 0.0)
    lower = jnp.where(iota((t, t), 0) >= iota((t, t), 1), 1.0, 0.0)
    c_row = jnp.dot(logs, upper, precision=HIGHEST, preferred_element_type=F32)
    c_col = lax.dot_general(
        lower, logs, (((1,), (1,)), ((), ())), precision=HIGHEST, preferred_element_type=F32
    )
    per_head = 128 // hd
    for h in range(heads):
        head = pl.ds(h * 128, 128)
        total = c_row[h : h + 1, t - 1 : t]
        r["ts"][h] = jnp.broadcast_to(total, (1, 128))
        weighted = k[:, head].astype(F32) * jnp.exp(total - c_col[:, h : h + 1])
        high, low = split2(weighted)
        product = (mm_tn(high, v[:, head]) + mm_tn(low, v[:, head])).astype(BF16)
        for i in range(per_head):
            r["ub"][h * per_head + i] = product[i * hd : (i + 1) * hd]

    pl.semaphore_wait(barrier, n - 1 + tp_n - 1)

    ub, ur, ts, tr, sb, se = (r[name] for name in ("ub", "ur", "ts", "tr", "sb", "se"))
    seq_peers(lambda p: send(ts.at[p // per_head], tr.at[s], m_s.at[0], m_r.at[0], (p, tp)))
    seq_peers(lambda p: send(ub.at[p], ur.at[s], m_s.at[1], m_r.at[1], (p, tp)))
    pending.append((tr.at[pl.ds(0, n - 1)], m_s.at[0]))
    pending.append((ur.at[pl.ds(0, n - 1)], m_s.at[1]))
    tr[s] = ts[s // per_head]
    ur[s] = ub[s]

    ids_r = idst[...]
    first, second = (to_column(ids_r[j : j + 1, :].astype(F32)) for j in range(2))
    picks = (first, second)
    names_lane = iota((t, n), 1).astype(F32)
    slots_c = []
    before = flag(iota((t, t), 1) < iota((t, t), 0))
    counts = mm(before, flag((first == names_lane) | (second == names_lane)))
    for j, pick, q_ref in ((0, first, r["q0"]), (1, second, r["q1"])):
        slot = jnp.sum(jnp.where(pick == names_lane, counts, 0.0), axis=1, keepdims=True)
        slots_c.append(slot)
        target = pick * PAD + slot
        q_ref[...] = flag(iota((t, n * PAD), 1).astype(F32) == target)
    first, second = ids_r[0:1, :], ids_r[1:2, :]
    names_sub = iota((n, t), 0)
    after = flag(iota((t, t), 0) < iota((t, t), 1))
    counts = mm(flag((first == names_sub) | (second == names_sub)), after)
    targets = []
    for pick in (first, second):
        slot = jnp.sum(jnp.where(pick == names_sub, counts, 0.0), axis=0, keepdims=True)
        targets.append(pick.astype(F32) * PAD + slot)
    place = iota((n * PAD, t), 0).astype(F32)
    r["pm"][...] = flag((place == targets[0]) | (place == targets[1]))

    causal = iota((t, t), 0) >= iota((t, t), 1)
    for h in range(heads):
        head = pl.ds(h * 128, 128)
        scores = mm_nt(q[:, head], k[:, head])
        gap = jnp.where(causal, c_col[:, h : h + 1] - c_row[h : h + 1, :], 0.0)
        intra = jnp.where(causal, scores * jnp.exp(gap), 0.0).astype(BF16)
        r["within"][:, head] = mm(intra, v[:, head])

    wait(tr.at[pl.ds(0, n - 1)], m_r.at[0])
    wait(ur.at[pl.ds(0, n - 1)], m_r.at[1])

    def scan(b, state):
        sb[b] = state.astype(BF16)
        return jnp.exp(tr[b]) * state + ur[b].astype(F32)

    lax.fori_loop(0, n, scan, jnp.zeros((hd, 128), F32))
    seq_peers(lambda p: send(sb.at[p], se.at[s], m_s.at[2], m_r.at[2], (p, tp)))
    pending.append((se.at[pl.ds(0, n - 1)], m_s.at[2]))
    se[s] = sb[s]
    wait(se.at[pl.ds(0, n - 1)], m_r.at[2])

    attended = []
    for h in range(heads):
        head = pl.ds(h * 128, 128)
        state = se[h * per_head : (h + 1) * per_head].reshape(128, 128)
        head_out = r["within"][:, head] + mm(q[:, head], state) * jnp.exp(c_col[:, h : h + 1])
        mean = jnp.mean(head_out * head_out, axis=1, keepdims=True)
        attended.append((head_out * lax.rsqrt(mean + EPSILON)).astype(BF16))
    attention = jnp.concatenate(attended, axis=1)

    ps1, pr1, ps2, pr2 = (r[name] for name in ("ps1", "pr1", "ps2", "pr2"))
    for copy in weights[: tp_n + 1]:
        copy.wait()
    for to in (opposite, ahead, behind, y):
        ps1[to] = mm(attention, r["owv"][to * CORES + 1 - core]).astype(BF16)
        send(ps1.at[to], pr1.at[to], r["p1_s"].at[to], r["p1_r"].at[to], partner)
        pending.append((ps1.at[to], r["p1_s"].at[to]))

    def chip_sum(to):
        mine = mm(attention, r["owv"][to * CORES + core])
        wait(pr1.at[to], r["p1_r"].at[to])
        return mine + pr1[to].astype(F32)

    rl1 = r["rl1"]
    halves = (pl.ds(0, t // 2), pl.ds(t // 2, t // 2))
    ps2[2] = chip_sum(opposite).astype(BF16)
    for i, (_, device) in enumerate(sides):
        send(ps2.at[2, halves[i]], rl1.at[i], r["l1_s"].at[i], r["l1_r"].at[i], device)
        pending.append((rl1.at[i], r["l1_s"].at[i]))
    with_relay = []
    for i, (to, device) in enumerate(sides):
        mine = chip_sum(to)
        ps2[i, halves[1 - i]] = mine[(1 - i) * (t // 2) : (2 - i) * (t // 2)].astype(BF16)
        piece = (i, halves[1 - i])
        send(ps2.at[piece], pr2.at[piece], r["p3_s"].at[i], r["p3_r"].at[i], device)
        pending.append((ps2.at[piece], r["p3_s"].at[i]))
        with_relay.append(mine[i * (t // 2) : (i + 1) * (t // 2)])
    for i, (_, device) in enumerate(sides):
        wait(rl1.at[i], r["l1_r"].at[i])
        piece = (i, halves[i])
        ps2[piece] = (with_relay[i] + rl1[i].astype(F32)).astype(BF16)
        send(ps2.at[piece], pr2.at[piece], r["p2_s"].at[i], r["p2_r"].at[i], device)
        pending.append((ps2.at[piece], r["p2_s"].at[i]))
    hidden = res[...].astype(F32) + chip_sum(y)
    for i in range(2):
        wait(pr2.at[i, halves[1 - i]], r["p3_r"].at[i])
        wait(pr2.at[i, halves[i]], r["p2_r"].at[i])
        hidden = hidden + pr2[i].astype(F32)

    dsp, xr, ret = r["dsp"], r["xr"], r["ret"]
    scaled = (hidden * mult[...][None, :]).astype(BF16)
    dsp[...] = mm(r["pm"][...], scaled).astype(BF16)

    def rows_of(index):
        return pl.ds(pl.multiple_of(index * PAD, PAD), PAD)

    home_group = [g for g, steps in enumerate(groups) if steps[0] == 0][0]
    home_slot = starts[home_group]

    def group_peers(g, sign, body):
        def step(j, carry):
            dz = groups[g][0]
            for i in range(1, len(groups[g])):
                dz = jnp.where(j < i * xs, dz, groups[g][i])
            dx = lax.rem(j, xs)
            pz = lax.rem(z + zs + sign * dz, zs)
            px = lax.rem(x + xs + sign * dx, xs)
            body(starts[g] + j, pz * xs + px)
            return carry

        lax.fori_loop(0 if g != home_group else 1, sizes[g], step, 0)

    for g in range(len(groups)):
        group_peers(
            g,
            1,
            lambda j, p, g=g: send(
                dsp.at[rows_of(p)], xr.at[rows_of(j)], r["x_s"].at[g], r["x_r"].at[g], (p, tp)
            ),
        )
    def group_ref(g):
        skip = 1 if g == home_group else 0
        return xr.at[pl.ds((starts[g] + skip) * PAD, (sizes[g] - skip) * PAD)]

    for g in range(len(groups)):
        pending.append((group_ref(g), r["x_s"].at[g]))
    xr[home_slot * PAD : (home_slot + 1) * PAD] = dsp[rows_of(s)]

    sqs, sqr = r["sqs"], r["sqr"]
    high, low = split2(hidden * hidden)
    ones = jnp.ones((8, w), BF16)
    sqs[...] = (mm_nt(ones, high) + mm_nt(ones, low))[0:1]
    tp_peers(lambda p: send(sqs, sqr.at[tp], m_s.at[3], m_r.at[3], (s, p)))
    pending.append((sqr.at[pl.ds(0, tp_n - 1)], m_s.at[3]))
    sqr[tp] = sqs[...]
    partial_logits = mm_nt(scaled, r["rwv"][...])
    wait(sqr.at[pl.ds(0, tp_n - 1)], m_r.at[3])
    square_sum = sqr[0]
    for u in range(1, tp_n):
        square_sum = square_sum + sqr[u]
    inverse = to_column(lax.rsqrt(square_sum / (w * tp_n) + EPSILON))
    factors = jnp.zeros((n, 128), F32)
    lane = iota((t, 128), 1).astype(F32)
    for pick, slot in zip(picks, slots_c):
        chosen = flag(pick == names_lane)
        rest = jnp.where(slot == lane, inverse, 0.0)
        for _ in range(3):
            piece = rest.astype(BF16)
            rest = rest - piece.astype(F32)
            factors = factors + mm_tn(chosen, piece)
    fs, fr = r["fs"], r["fr"]
    for i in range(n):
        fs[i] = factors[i : i + 1]
    for g in range(len(groups)):
        group_peers(
            g,
            1,
            lambda j, p, g=g: send(
                fs.at[p], fr.at[j], m_s.at[6], m_r.at[6], (p, tp)
            ),
        )
    pending.append((fr.at[pl.ds(0, n - 1)], m_s.at[6]))
    fr[home_slot] = fs[s]

    cs, cr = r["cs"], r["cr"]
    logits = partial_logits * inverse
    for j in range(2):
        chosen = jnp.where(picks[j] == names_lane, logits, 0.0)
        cs[j] = to_row(jnp.sum(chosen, axis=1, keepdims=True))
    tp_peers(lambda p: send(cs, cr.at[tp], m_s.at[4], m_r.at[4], (s, p)))
    pending.append((cr.at[pl.ds(0, tp_n - 1)], m_s.at[4]))
    cr[tp] = cs[...]

    xg, mb, ps, pr = (r[name] for name in ("xg", "mb", "ps", "pr"))
    ys, yr, rl, hs = (r[name] for name in ("ys", "yr", "rl", "hs"))

    def compaction(count):
        row, lane = iota((count * CAP, count * PAD), 0), iota((count * CAP, count * PAD), 1)
        block = (row * 2731) >> 16
        return flag(lane == block * PAD + (row - block * CAP))

    def expansion(count):
        row, lane = iota((count * PAD, count * CAP), 0), iota((count * PAD, count * CAP), 1)
        block = (lane * 2731) >> 16
        return flag(row == block * PAD + (lane - block * CAP))

    def slots_of(g, unit):
        return pl.ds(starts[g] * unit, sizes[g] * unit)

    def rows_in(g):
        return slots_of(g, CAP)

    def half_rows(g, i):
        return pl.ds(starts[g] * CAP + i * sizes[g] * CAP // 2, sizes[g] * CAP // 2)

    own_half = pl.ds(pl.multiple_of(core * w, w), w)
    other_half = pl.ds(pl.multiple_of((1 - core) * w, w), w)
    origins = (behind, ahead)

    def spread_out(g):
        wait(group_ref(g), r["x_r"].at[g])
        packed = mm(compaction(sizes[g]), xr[slots_of(g, PAD)]).astype(BF16)
        for side in range(CORES):

            @pl.when(core == side)
            def _(side=side):
                xg[y, rows_in(g), side * w : (side + 1) * w] = packed

        piece = xg.at[y, rows_in(g), own_half]
        for i, (_, device) in enumerate(sides):
            send(piece, piece, r["a_s"].at[g, i], r["a_r"].at[g, i], device)
            pending.append((piece, r["a_s"].at[g, i]))
        send(piece, piece, r["b_s"].at[g, y], r["b_r"].at[g, y], partner)
        pending.append((piece, r["b_s"].at[g, y]))

    def pass_over(g, block):
        piece = xg.at[block, rows_in(g), own_half]
        send(piece, piece, r["b_s"].at[g, block], r["b_r"].at[g, block], partner)
        pending.append((piece, r["b_s"].at[g, block]))

    def pass_on(g):
        for i, (_, device) in enumerate(sides):
            wait(xg.at[origins[i], rows_in(g), own_half], r["a_r"].at[g, i])
            piece = xg.at[origins[i], half_rows(g, i), own_half]
            send(piece, piece, r["f_s"].at[g, i], r["f_r"].at[g, i], device)
            pending.append((piece, r["f_s"].at[g, i]))
            pass_over(g, origins[i])

    def pass_far(g):
        for i in range(2):
            wait(xg.at[opposite, half_rows(g, i), own_half], r["f_r"].at[g, i])
        pass_over(g, opposite)

    waited = []

    def expert(g):
        for i in range(ys_n):
            wait(xg.at[i, rows_in(g), other_half], r["b_r"].at[g, i])
        total = mm(xg[0, rows_in(g)], r["upv"][0])
        for i in range(1, ys_n):
            total = total + mm(xg[i, rows_in(g)], r["upv"][i])
        if not waited:
            wait(fr.at[pl.ds(0, n - 1)], m_r.at[6])
            waited.append(g)
        mine = range(starts[g], starts[g] + sizes[g])
        spots = [jnp.broadcast_to(fr[j], (CAP, 128)) for j in mine]
        spots = jnp.concatenate(spots, axis=0)
        spot_row, spot_lane = iota((sizes[g] * CAP, 128), 0), iota((sizes[g] * CAP, 128), 1)
        spot_row = spot_row - ((spot_row * 2731) >> 16) * CAP
        total = total * jnp.sum(jnp.where(spot_lane == spot_row, spots, 0.0), axis=1, keepdims=True)
        hidden_rows = (total / (1.0 + jnp.exp(-total))).astype(BF16)
        for i in range(ys_n):
            part = mm(hidden_rows, r["dnv"][i])
            left, right = part[:, :w], part[:, w:]
            mb[i, rows_in(g)] = jnp.where(core == 0, left, right)
            ps[i, rows_in(g)] = jnp.where(core == 0, right, left).astype(BF16)
            piece = (i, rows_in(g))
            send(ps.at[piece], pr.at[piece], r["c_s"].at[g, i], r["c_r"].at[g, i], partner)
            pending.append((ps.at[piece], r["c_s"].at[g, i]))

    def chip_rows(g, to, part):
        return mb[to, part] + pr[to, part].astype(F32)

    def sum_far(g):
        for i in range(ys_n):
            wait(pr.at[i, rows_in(g)], r["c_r"].at[g, i])
        for i, (_, device) in enumerate(sides):
            part = half_rows(g, i)
            ys[2, part] = chip_rows(g, opposite, part).astype(BF16)
            send(ys.at[2, part], rl.at[part], r["l_s"].at[g, i], r["l_r"].at[g, i], device)
            pending.append((ys.at[2, part], r["l_s"].at[g, i]))
        for i, (to, device) in enumerate(sides):
            part = half_rows(g, 1 - i)
            ys[i, part] = chip_rows(g, to, part).astype(BF16)
            send(ys.at[i, part], yr.at[i, part], r["e_s"].at[g, i], r["e_r"].at[g, i], device)
            pending.append((ys.at[i, part], r["e_s"].at[g, i]))

    def sum_near(g):
        for i, (to, device) in enumerate(sides):
            part = half_rows(g, i)
            wait(rl.at[part], r["l_r"].at[g, i])
            ys[i, part] = (chip_rows(g, to, part) + rl[part].astype(F32)).astype(BF16)
            send(ys.at[i, part], yr.at[i, part], r["d_s"].at[g, i], r["d_r"].at[g, i], device)
            pending.append((ys.at[i, part], r["d_s"].at[g, i]))

    def home(g):
        total = chip_rows(g, y, rows_in(g))
        for i in range(2):
            wait(yr.at[i, half_rows(g, 1 - i)], r["e_r"].at[g, i])
            wait(yr.at[i, half_rows(g, i)], r["d_r"].at[g, i])
            total = total + yr[i, rows_in(g)].astype(F32)
        hs[slots_of(g, PAD)] = mm(expansion(sizes[g]), total.astype(BF16)).astype(BF16)
        group_peers(
            g,
            -1,
            lambda j, p: send(
                hs.at[rows_of(j)], ret.at[rows_of(s)], r["h_s"].at[g], m_r.at[5], (p, tp)
            ),
        )
        pending.append((group_ref(g), r["h_s"].at[g]))
        if g == home_group:
            ret[rows_of(s)] = hs[home_slot * PAD : (home_slot + 1) * PAD]

    for copy in weights[tp_n + 1 :]:
        copy.wait()
    stages = (spread_out, pass_on, pass_far, expert, sum_far, sum_near, home)
    todo = {g: list(stages) for g in range(len(groups))}
    for g in c["order"]:
        todo[g].pop(0)(g)

    wait(cr.at[pl.ds(0, tp_n - 1)], m_r.at[4])
    gates = []
    for j in range(2):
        logit = cr[0, j]
        for u in range(1, tp_n):
            logit = logit + cr[u, j]
        gates.append(jax.nn.sigmoid(logit))
    both = gates[0] + gates[1]
    shares = [to_column(gate / both) for gate in gates]
    wait(ret.at[pl.ds(0, (n - 1) * PAD)], m_r.at[5])
    returned = ret[...]
    mix = shares[0] * mm(r["q0"][...], returned) + shares[1] * mm(r["q1"][...], returned)
    out[...] = (hidden + mix).astype(BF16)

    for ref, sem in pending:
        wait(ref, sem)


GROUPS = {8: [(1, 7), (2, 6), (3, 5), (0, 4)]}
ORDERS = {8: [0, 1, 0, 1, 2, 0, 3, 0, 2, 0, 1, 1, 2, 3, 1, 2, 0, 1, 3, 2, 3, 0, 1, 2, 3, 2, 3, 3]}


def stepped(count, stages=7):
    return [
        step - lag
        for step in range(count + stages - 1)
        for lag in range(stages)
        if 0 <= step - lag < count
    ]


def body(
    sizes,
    queries,
    keys,
    values,
    log_decay,
    residual,
    out_weight,
    prenorm_multiplier,
    router_weight,
    picked_unit_indices,
    expert_up_weight,
    down_weight,
):
    n, xs, zs, ys = sizes
    half = zs // 2
    groups = GROUPS.get(zs) or [(d, zs - d) for d in range(1, half)] + [(0, half)]
    order = ORDERS.get(zs) or stepped(len(groups))
    heads = log_decay.shape[0]
    c = dict(
        n=n,
        x=xs,
        z=zs,
        y=ys,
        groups=groups,
        order=order,
        g=len(groups),
        heads=heads,
        t=queries.shape[0],
        a=queries.shape[1],
        w=residual.shape[1],
        f=expert_up_weight.shape[2],
        hd=heads * 128 // n,
    )
    scratch = scratch_of(c)
    vmem, anywhere = pl.BlockSpec(memory_space=pltpu.VMEM), pl.BlockSpec(memory_space=pl.ANY)
    return pl.pallas_call(
        functools.partial(kernel, c, list(scratch)),
        out_shape=jax.ShapeDtypeStruct(residual.shape, BF16),
        in_specs=[vmem] * 7 + [anywhere] * 4,
        out_specs=vmem,
        scratch_shapes=list(scratch.values()),
        compiler_params=pltpu.CompilerParams(
            collective_id=0, has_side_effects=True, vmem_limit_bytes=56 * 1024 * 1024
        ),
    )(
        queries,
        keys,
        values,
        log_decay,
        residual,
        prenorm_multiplier,
        picked_unit_indices.T,
        out_weight,
        router_weight.T,
        expert_up_weight,
        down_weight,
    )


def solution(mesh):
    n = mesh.shape["seq"]
    xs = 4 if n % 4 == 0 and n > 4 else 2
    sizes = (n, xs, n // xs, mesh.shape["tp"] // CORES)
    in_specs = (
        P("seq", "tp"),
        P("seq", "tp"),
        P("seq", "tp"),
        P("tp", "seq"),
        P("seq", "tp"),
        P("tp", None),
        P("tp"),
        P(),
        P("seq", None),
        P("seq", None, "tp"),
        P("seq", "tp", None),
    )
    return jax.shard_map(
        functools.partial(body, sizes),
        mesh=mesh,
        in_specs=in_specs,
        out_specs=P("seq", "tp"),
        check_vma=False,
    )
```

```python
import functools

import jax
import jax.numpy as jnp
from jax import lax
from jax.experimental import pallas as pl
from jax.experimental.pallas import tpu as pltpu
from jax.sharding import PartitionSpec as P

EPSILON = 1e-05
MESH = pl.DeviceIdType.MESH
F32, BF16 = jnp.float32, jnp.bfloat16
HIGHEST = lax.Precision.HIGHEST
CAP = 24
TILE = 16
PIECES = 5
CORES = 2


def mm(a, b):
    return jnp.dot(a, b, preferred_element_type=F32)


def mm_nt(a, b):
    return lax.dot_general(a, b, (((1,), (1,)), ((), ())), preferred_element_type=F32)


def mm_tn(a, b):
    return lax.dot_general(a, b, (((0,), (0,)), ((), ())), preferred_element_type=F32)


def iota(shape, dim):
    return lax.broadcasted_iota(jnp.int32, shape, dim)


def flag(mask):
    return jnp.where(mask, 1.0, 0.0).astype(BF16)


def split2(x):
    high = x.astype(BF16)
    return high, (x - high.astype(F32)).astype(BF16)


def to_column(row):
    n = row.shape[1]
    eye = iota((n, n), 0) == iota((n, n), 1)
    return jnp.sum(jnp.where(eye, row, 0.0), axis=1, keepdims=True)


def to_row(column):
    n = column.shape[0]
    eye = iota((n, n), 0) == iota((n, n), 1)
    return jnp.sum(jnp.where(eye, column, 0.0), axis=0, keepdims=True)


def places(block, slot):
    late = slot >= TILE
    base = block * TILE + slot
    nowhere = jnp.full(base.shape, -1, base.dtype)
    return (
        jnp.where(late, nowhere, base),
        jnp.where(late, base - TILE, nowhere),
        jnp.where(late, base - TILE // 2, nowhere),
    )


def to_pieces(parts, rows, out, where):
    head = mm(parts[0], rows).astype(BF16)
    for i in range(3):
        out[i, where] = head[:, i * 128 : (i + 1) * 128]
    tail = mm(parts[1], rows[:, 0:128]) + mm(parts[2], rows[:, 128:256])
    out[3, where] = tail.astype(BF16)
    out[4, where] = mm(parts[1], rows[:, 256:384]).astype(BF16)


def from_pieces(parts, pieces, where):
    head = jnp.concatenate([pieces[i, where] for i in range(3)], axis=1)
    third, fourth = pieces[3, where], pieces[4, where]
    tail = [mm(parts[1], third), mm(parts[2], third), mm(parts[1], fourth)]
    return mm(parts[0], head) + jnp.concatenate(tail, axis=1)


def send(src, dst, send_sem, recv_sem, device):
    pltpu.make_async_remote_copy(
        src_ref=src,
        dst_ref=dst,
        send_sem=send_sem,
        recv_sem=recv_sem,
        device_id=device,
        device_id_type=MESH,
    ).start()


def wait(ref, sem):
    pltpu.make_async_copy(ref, ref, sem).wait()


def scratch_of(c):
    n, y, g, w, t, hd = c["n"], c["y"], c["g"], c["w"], c["t"], c["hd"]
    tp, f, rows = y * CORES, c["f"], n * CAP
    dma = pltpu.SemaphoreType.DMA
    return dict(
        owv=pltpu.VMEM((tp, c["a"], w), BF16),
        rwv=pltpu.VMEM((n, w), BF16),
        upv=pltpu.VMEM((y, CORES * w, f), BF16),
        dnv=pltpu.VMEM((y, f, CORES * w), BF16),
        ub=pltpu.VMEM((n, hd, 128), BF16),
        ur=pltpu.VMEM((n, hd, 128), BF16),
        ts=pltpu.VMEM((c["heads"], 1, 128), F32),
        tr=pltpu.VMEM((n, 1, 128), F32),
        sb=pltpu.VMEM((n, hd, 128), BF16),
        se=pltpu.VMEM((n, hd, 128), BF16),
        within=pltpu.VMEM((t, c["a"]), F32),
        ps1=pltpu.VMEM((y, t, w), BF16),
        pr1=pltpu.VMEM((y, t, w), BF16),
        ps2=pltpu.VMEM((y, t, w), BF16),
        pr2=pltpu.VMEM((y, t, w), BF16),
        rl1=pltpu.VMEM((2, t // 2, w), BF16),
        sqs=pltpu.VMEM((1, t), F32),
        sqr=pltpu.VMEM((tp, 1, t), F32),
        fs=pltpu.VMEM((n, 1, 128), F32),
        fr=pltpu.VMEM((n, 1, 128), F32),
        cs=pltpu.VMEM((2, 1, t), F32),
        cr=pltpu.VMEM((tp, 2, 1, t), F32),
        pm=pltpu.VMEM((3, n * TILE, t), BF16),
        q=pltpu.VMEM((2, 3, t, n * TILE), BF16),
        dsp=pltpu.VMEM((PIECES, n * TILE, 128), BF16),
        xr=pltpu.VMEM((PIECES, n * TILE, 128), BF16),
        xg=pltpu.VMEM((tp, rows, w), BF16),
        mb=pltpu.VMEM((y, rows, w), F32),
        ps=pltpu.VMEM((y, rows, w), BF16),
        pr=pltpu.VMEM((y, rows, w), BF16),
        ys=pltpu.VMEM((y, rows, w), BF16),
        yr=pltpu.VMEM((y, rows, w), BF16),
        rl=pltpu.VMEM((rows, w), BF16),
        hs=pltpu.VMEM((PIECES, n * TILE, 128), BF16),
        ret=pltpu.VMEM((PIECES, n * TILE, 128), BF16),
        w_ow=dma((tp,)),
        w_up=dma((y,)),
        w_dn=dma((y,)),
        w_rw=dma((1,)),
        m_s=dma((8,)),
        m_r=dma((8,)),
        p1_s=dma((y,)),
        p1_r=dma((y,)),
        p2_s=dma((y,)),
        p2_r=dma((y,)),
        p3_s=dma((2,)),
        p3_r=dma((2,)),
        l1_s=dma((2,)),
        l1_r=dma((2,)),
        x_s=dma((g,)),
        x_r=dma((g,)),
        a_s=dma((g, y)),
        a_r=dma((g, y)),
        b_s=dma((g, y)),
        b_r=dma((g, y)),
        c_s=dma((g, y)),
        c_r=dma((g, y)),
        d_s=dma((g, y)),
        d_r=dma((g, y)),
        e_s=dma((g, 2)),
        e_r=dma((g, 2)),
        f_s=dma((g, 2)),
        f_r=dma((g, 2)),
        l_s=dma((g, 2)),
        l_r=dma((g, 2)),
        h_s=dma((g,)),
    )


def kernel(c, names, *refs):
    (q, k, v, ld, res, mult, idst, ow, rw, up, dn, out) = refs[:12]
    r = dict(zip(names, refs[12:]))
    n, xs, zs, ys_n, groups = c["n"], c["x"], c["z"], c["y"], c["groups"]
    heads, t, w, hd, tp_n = c["heads"], c["t"], c["w"], c["hd"], c["y"] * CORES
    starts = [xs * sum(len(steps) for steps in groups[:g]) for g in range(len(groups))]
    sizes = [xs * len(steps) for steps in groups]
    s, tp = lax.axis_index("seq"), lax.axis_index("tp")
    z, x = s // xs, lax.rem(s, xs)
    y, core = tp // CORES, lax.rem(tp, CORES)
    partner = (s, y * CORES + 1 - core)
    ahead, behind, opposite = (lax.rem(y + d, ys_n) for d in (1, 3, 2))
    sides = ((ahead, (s, ahead * CORES + core)), (behind, (s, behind * CORES + core)))
    m_s, m_r = r["m_s"], r["m_r"]

    def seq_peers(body):
        def step(i, carry):
            distance = (n - i + 1) // 2
            body(lax.rem(s + jnp.where(lax.rem(i, 2) == 1, distance, n - distance), n))
            return carry

        lax.fori_loop(1, n, step, 0)

    def tp_peers(body):
        def step(i, carry):
            body(lax.rem(tp + i, tp_n))
            return carry

        lax.fori_loop(1, tp_n, step, 0)

    pending = []
    barrier = pltpu.get_barrier_semaphore()
    seq_peers(
        lambda p: pl.semaphore_signal(barrier, inc=1, device_id=(p, tp), device_id_type=MESH)
    )
    tp_peers(lambda p: pl.semaphore_signal(barrier, inc=1, device_id=(s, p), device_id_type=MESH))

    weights = []
    for u in range(tp_n):
        weights.append(
            pltpu.make_async_copy(ow.at[:, pl.ds(u * w, w)], r["owv"].at[u], r["w_ow"].at[u])
        )
    weights.append(
        pltpu.make_async_copy(
            rw.at[:, pl.ds(pl.multiple_of(tp * w, w), w)], r["rwv"], r["w_rw"].at[0]
        )
    )
    for i in range(ys_n):
        part = pl.ds(i * CORES * w, CORES * w)
        weights.append(
            pltpu.make_async_copy(up.at[0, part, :], r["upv"].at[i], r["w_up"].at[i])
        )
    for i in range(ys_n):
        part = pl.ds(i * CORES * w, CORES * w)
        weights.append(
            pltpu.make_async_copy(dn.at[0, :, part], r["dnv"].at[i], r["w_dn"].at[i])
        )
    for copy in weights:
        copy.start()

    logs = ld[...]
    upper = jnp.where(iota((t, t), 0) <= iota((t, t), 1), 1.0, 0.0)
    lower = jnp.where(iota((t, t), 0) >= iota((t, t), 1), 1.0, 0.0)
    c_row = jnp.dot(logs, upper, precision=HIGHEST, preferred_element_type=F32)
    c_col = lax.dot_general(
        lower, logs, (((1,), (1,)), ((), ())), precision=HIGHEST, preferred_element_type=F32
    )
    per_head = 128 // hd
    for h in range(heads):
        head = pl.ds(h * 128, 128)
        total = c_row[h : h + 1, t - 1 : t]
        r["ts"][h] = jnp.broadcast_to(total, (1, 128))
        weighted = k[:, head].astype(F32) * jnp.exp(total - c_col[:, h : h + 1])
        high, low = split2(weighted)
        product = (mm_tn(high, v[:, head]) + mm_tn(low, v[:, head])).astype(BF16)
        for i in range(per_head):
            r["ub"][h * per_head + i] = product[i * hd : (i + 1) * hd]

    pl.semaphore_wait(barrier, n - 1 + tp_n - 1)

    ub, ur, ts, tr, sb, se = (r[name] for name in ("ub", "ur", "ts", "tr", "sb", "se"))
    seq_peers(lambda p: send(ts.at[p // per_head], tr.at[s], m_s.at[0], m_r.at[0], (p, tp)))
    seq_peers(lambda p: send(ub.at[p], ur.at[s], m_s.at[1], m_r.at[1], (p, tp)))
    pending.append((tr.at[pl.ds(0, n - 1)], m_s.at[0]))
    pending.append((ur.at[pl.ds(0, n - 1)], m_s.at[1]))
    tr[s] = ts[s // per_head]
    ur[s] = ub[s]

    ids_r = idst[...]
    first, second = (to_column(ids_r[j : j + 1, :].astype(F32)) for j in range(2))
    picks = (first, second)
    names_lane = iota((t, n), 1).astype(F32)
    slots_c = []
    before = flag(iota((t, t), 1) < iota((t, t), 0))
    counts = mm(before, flag((first == names_lane) | (second == names_lane)))
    for j, pick in enumerate(picks):
        slot = jnp.sum(jnp.where(pick == names_lane, counts, 0.0), axis=1, keepdims=True)
        slots_c.append(slot)
        for i, target in enumerate(places(pick, slot)):
            r["q"][j, i] = flag(iota((t, n * TILE), 1).astype(F32) == target)
    first, second = ids_r[0:1, :], ids_r[1:2, :]
    names_sub = iota((n, t), 0)
    after = flag(iota((t, t), 0) < iota((t, t), 1))
    counts = mm(flag((first == names_sub) | (second == names_sub)), after)
    targets = []
    for pick in (first, second):
        slot = jnp.sum(jnp.where(pick == names_sub, counts, 0.0), axis=0, keepdims=True)
        targets.append(places(pick.astype(F32), slot))
    place = iota((n * TILE, t), 0).astype(F32)
    for i in range(3):
        r["pm"][i] = flag((place == targets[0][i]) | (place == targets[1][i]))

    causal = iota((t, t), 0) >= iota((t, t), 1)
    for h in range(heads):
        head = pl.ds(h * 128, 128)
        scores = mm_nt(q[:, head], k[:, head])
        gap = jnp.where(causal, c_col[:, h : h + 1] - c_row[h : h + 1, :], 0.0)
        intra = jnp.where(causal, scores * jnp.exp(gap), 0.0).astype(BF16)
        r["within"][:, head] = mm(intra, v[:, head])

    wait(tr.at[pl.ds(0, n - 1)], m_r.at[0])
    wait(ur.at[pl.ds(0, n - 1)], m_r.at[1])

    def scan(b, state):
        sb[b] = state.astype(BF16)
        return jnp.exp(tr[b]) * state + ur[b].astype(F32)

    lax.fori_loop(0, n, scan, jnp.zeros((hd, 128), F32))
    seq_peers(lambda p: send(sb.at[p], se.at[s], m_s.at[2], m_r.at[2], (p, tp)))
    pending.append((se.at[pl.ds(0, n - 1)], m_s.at[2]))
    se[s] = sb[s]
    wait(se.at[pl.ds(0, n - 1)], m_r.at[2])

    attended = []
    for h in range(heads):
        head = pl.ds(h * 128, 128)
        state = se[h * per_head : (h + 1) * per_head].reshape(128, 128)
        head_out = r["within"][:, head] + mm(q[:, head], state) * jnp.exp(c_col[:, h : h + 1])
        mean = jnp.mean(head_out * head_out, axis=1, keepdims=True)
        attended.append((head_out * lax.rsqrt(mean + EPSILON)).astype(BF16))
    attention = jnp.concatenate(attended, axis=1)

    ps1, pr1, ps2, pr2 = (r[name] for name in ("ps1", "pr1", "ps2", "pr2"))
    for copy in weights[: tp_n + 1]:
        copy.wait()
    for to in (opposite, ahead, behind, y):
        ps1[to] = mm(attention, r["owv"][to * CORES + 1 - core]).astype(BF16)
        send(ps1.at[to], pr1.at[to], r["p1_s"].at[to], r["p1_r"].at[to], partner)
        pending.append((ps1.at[to], r["p1_s"].at[to]))

    def chip_sum(to):
        mine = mm(attention, r["owv"][to * CORES + core])
        wait(pr1.at[to], r["p1_r"].at[to])
        return mine + pr1[to].astype(F32)

    rl1 = r["rl1"]
    halves = (pl.ds(0, t // 2), pl.ds(t // 2, t // 2))
    ps2[2] = chip_sum(opposite).astype(BF16)
    for i, (_, device) in enumerate(sides):
        send(ps2.at[2, halves[i]], rl1.at[i], r["l1_s"].at[i], r["l1_r"].at[i], device)
        pending.append((rl1.at[i], r["l1_s"].at[i]))
    with_relay = []
    for i, (to, device) in enumerate(sides):
        mine = chip_sum(to)
        ps2[i, halves[1 - i]] = mine[(1 - i) * (t // 2) : (2 - i) * (t // 2)].astype(BF16)
        piece = (i, halves[1 - i])
        send(ps2.at[piece], pr2.at[piece], r["p3_s"].at[i], r["p3_r"].at[i], device)
        pending.append((ps2.at[piece], r["p3_s"].at[i]))
        with_relay.append(mine[i * (t // 2) : (i + 1) * (t // 2)])
    for i, (_, device) in enumerate(sides):
        wait(rl1.at[i], r["l1_r"].at[i])
        piece = (i, halves[i])
        ps2[piece] = (with_relay[i] + rl1[i].astype(F32)).astype(BF16)
        send(ps2.at[piece], pr2.at[piece], r["p2_s"].at[i], r["p2_r"].at[i], device)
        pending.append((ps2.at[piece], r["p2_s"].at[i]))
    hidden = res[...].astype(F32) + chip_sum(y)
    for i in range(2):
        wait(pr2.at[i, halves[1 - i]], r["p3_r"].at[i])
        wait(pr2.at[i, halves[i]], r["p2_r"].at[i])
        hidden = hidden + pr2[i].astype(F32)

    dsp, xr, ret = r["dsp"], r["xr"], r["ret"]
    scaled = (hidden * mult[...][None, :]).astype(BF16)
    to_pieces([r["pm"][i] for i in range(3)], scaled, dsp, pl.ds(0, n * TILE))

    def rows_of(index):
        return pl.ds(pl.multiple_of(index * TILE, TILE), TILE)

    home_group = [g for g, steps in enumerate(groups) if steps[0] == 0][0]
    home_slot = starts[home_group]

    def group_peers(g, sign, body):
        def step(j, carry):
            dz = groups[g][0]
            for i in range(1, len(groups[g])):
                dz = jnp.where(j < i * xs, dz, groups[g][i])
            dx = lax.rem(j, xs)
            pz = lax.rem(z + zs + sign * dz, zs)
            px = lax.rem(x + xs + sign * dx, xs)
            body(starts[g] + j, pz * xs + px)
            return carry

        lax.fori_loop(0 if g != home_group else 1, sizes[g], step, 0)

    for g in range(len(groups)):
        group_peers(
            g,
            1,
            lambda j, p, g=g: send(
                dsp.at[:, rows_of(p)], xr.at[:, rows_of(j)], r["x_s"].at[g], r["x_r"].at[g], (p, tp)
            ),
        )
    def group_ref(g):
        skip = 1 if g == home_group else 0
        return xr.at[:, pl.ds((starts[g] + skip) * TILE, (sizes[g] - skip) * TILE)]

    for g in range(len(groups)):
        pending.append((group_ref(g), r["x_s"].at[g]))
    xr[:, home_slot * TILE : (home_slot + 1) * TILE] = dsp[:, rows_of(s)]

    sqs, sqr = r["sqs"], r["sqr"]
    high, low = split2(hidden * hidden)
    ones = jnp.ones((8, w), BF16)
    sqs[...] = (mm_nt(ones, high) + mm_nt(ones, low))[0:1]
    tp_peers(lambda p: send(sqs, sqr.at[tp], m_s.at[3], m_r.at[3], (s, p)))
    pending.append((sqr.at[pl.ds(0, tp_n - 1)], m_s.at[3]))
    sqr[tp] = sqs[...]
    partial_logits = mm_nt(scaled, r["rwv"][...])
    wait(sqr.at[pl.ds(0, tp_n - 1)], m_r.at[3])
    square_sum = sqr[0]
    for u in range(1, tp_n):
        square_sum = square_sum + sqr[u]
    inverse = to_column(lax.rsqrt(square_sum / (w * tp_n) + EPSILON))
    factors = jnp.zeros((n, 128), F32)
    lane = iota((t, 128), 1).astype(F32)
    for pick, slot in zip(picks, slots_c):
        chosen = flag(pick == names_lane)
        rest = jnp.where(slot == lane, inverse, 0.0)
        for _ in range(3):
            piece = rest.astype(BF16)
            rest = rest - piece.astype(F32)
            factors = factors + mm_tn(chosen, piece)
    fs, fr = r["fs"], r["fr"]
    for i in range(n):
        fs[i] = factors[i : i + 1]
    for g in range(len(groups)):
        group_peers(
            g,
            1,
            lambda j, p, g=g: send(
                fs.at[p], fr.at[j], m_s.at[6], m_r.at[6], (p, tp)
            ),
        )
    pending.append((fr.at[pl.ds(0, n - 1)], m_s.at[6]))
    fr[home_slot] = fs[s]

    cs, cr = r["cs"], r["cr"]
    logits = partial_logits * inverse
    for j in range(2):
        chosen = jnp.where(picks[j] == names_lane, logits, 0.0)
        cs[j] = to_row(jnp.sum(chosen, axis=1, keepdims=True))
    tp_peers(lambda p: send(cs, cr.at[tp], m_s.at[4], m_r.at[4], (s, p)))
    pending.append((cr.at[pl.ds(0, tp_n - 1)], m_s.at[4]))
    cr[tp] = cs[...]

    xg, mb, ps, pr = (r[name] for name in ("xg", "mb", "ps", "pr"))
    ys, yr, rl, hs = (r[name] for name in ("ys", "yr", "rl", "hs"))

    def compaction(count):
        row, lane = iota((count * CAP, count * TILE), 0), iota((count * CAP, count * TILE), 1)
        block = (row * 2731) >> 16
        return [flag(lane == place) for place in places(block, row - block * CAP)]

    def expansion(count):
        row, lane = iota((count * TILE, count * CAP), 0), iota((count * TILE, count * CAP), 1)
        block = (lane * 2731) >> 16
        return [flag(row == place) for place in places(block, lane - block * CAP)]

    def slots_of(g, unit):
        return pl.ds(starts[g] * unit, sizes[g] * unit)

    def rows_in(g):
        return slots_of(g, CAP)

    def half_rows(g, i):
        return pl.ds(starts[g] * CAP + i * sizes[g] * CAP // 2, sizes[g] * CAP // 2)

    origins = (behind, ahead)

    def spread_out(g):
        wait(group_ref(g), r["x_r"].at[g])
        packed = from_pieces(compaction(sizes[g]), xr, slots_of(g, TILE)).astype(BF16)
        xg[tp, rows_in(g)] = packed
        piece = xg.at[tp, rows_in(g)]
        for i, (_, device) in enumerate(sides):
            send(piece, piece, r["a_s"].at[g, i], r["a_r"].at[g, i], device)
            pending.append((piece, r["a_s"].at[g, i]))
        if g in c["direct"]:
            across = (s, opposite * CORES + core)
            send(piece, piece, r["a_s"].at[g, 2], r["a_r"].at[g, 2], across)
            pending.append((piece, r["a_s"].at[g, 2]))
        send(piece, piece, r["b_s"].at[g, y], r["b_r"].at[g, y], partner)
        pending.append((piece, r["b_s"].at[g, y]))

    def pass_over(g, block):
        piece = xg.at[block * CORES + core, rows_in(g)]
        send(piece, piece, r["b_s"].at[g, block], r["b_r"].at[g, block], partner)
        pending.append((piece, r["b_s"].at[g, block]))

    def pass_on(g):
        for i, (_, device) in enumerate(sides):
            wait(xg.at[origins[i] * CORES + core, rows_in(g)], r["a_r"].at[g, i])
            if g not in c["direct"]:
                piece = xg.at[origins[i] * CORES + core, half_rows(g, i)]
                send(piece, piece, r["f_s"].at[g, i], r["f_r"].at[g, i], device)
                pending.append((piece, r["f_s"].at[g, i]))
            pass_over(g, origins[i])

    def pass_far(g):
        if g in c["direct"]:
            wait(xg.at[opposite * CORES + core, rows_in(g)], r["a_r"].at[g, 2])
        else:
            for i in range(2):
                wait(xg.at[opposite * CORES + core, half_rows(g, i)], r["f_r"].at[g, i])
        pass_over(g, opposite)

    waited = []

    def expert(g):
        for i in range(ys_n):
            wait(xg.at[i * CORES + 1 - core, rows_in(g)], r["b_r"].at[g, i])
        total = jnp.zeros((sizes[g] * CAP, c["f"]), F32)
        for i in range(ys_n):
            both = [xg[i * CORES + side, rows_in(g)] for side in range(CORES)]
            total = total + mm(jnp.concatenate(both, axis=1), r["upv"][i])
        if not waited:
            wait(fr.at[pl.ds(0, n - 1)], m_r.at[6])
            waited.append(g)
        mine = range(starts[g], starts[g] + sizes[g])
        spots = [jnp.broadcast_to(fr[j], (CAP, 128)) for j in mine]
        spots = jnp.concatenate(spots, axis=0)
        spot_row, spot_lane = iota((sizes[g] * CAP, 128), 0), iota((sizes[g] * CAP, 128), 1)
        spot_row = spot_row - ((spot_row * 2731) >> 16) * CAP
        total = total * jnp.sum(jnp.where(spot_lane == spot_row, spots, 0.0), axis=1, keepdims=True)
        hidden_rows = (total / (1.0 + jnp.exp(-total))).astype(BF16)
        for i in range(ys_n):
            part = mm(hidden_rows, r["dnv"][i])
            left, right = part[:, :w], part[:, w:]
            mb[i, rows_in(g)] = jnp.where(core == 0, left, right)
            ps[i, rows_in(g)] = jnp.where(core == 0, right, left).astype(BF16)
            piece = (i, rows_in(g))
            send(ps.at[piece], pr.at[piece], r["c_s"].at[g, i], r["c_r"].at[g, i], partner)
            pending.append((ps.at[piece], r["c_s"].at[g, i]))

    def chip_rows(g, to, part):
        return mb[to, part] + pr[to, part].astype(F32)

    def sum_far(g):
        for i in range(ys_n):
            wait(pr.at[i, rows_in(g)], r["c_r"].at[g, i])
        for i, (_, device) in enumerate(sides):
            part = half_rows(g, i)
            ys[2, part] = chip_rows(g, opposite, part).astype(BF16)
            send(ys.at[2, part], rl.at[part], r["l_s"].at[g, i], r["l_r"].at[g, i], device)
            pending.append((ys.at[2, part], r["l_s"].at[g, i]))
        for i, (to, device) in enumerate(sides):
            part = half_rows(g, 1 - i)
            ys[i, part] = chip_rows(g, to, part).astype(BF16)
            send(ys.at[i, part], yr.at[i, part], r["e_s"].at[g, i], r["e_r"].at[g, i], device)
            pending.append((ys.at[i, part], r["e_s"].at[g, i]))

    def sum_near(g):
        for i, (to, device) in enumerate(sides):
            part = half_rows(g, i)
            wait(rl.at[part], r["l_r"].at[g, i])
            ys[i, part] = (chip_rows(g, to, part) + rl[part].astype(F32)).astype(BF16)
            send(ys.at[i, part], yr.at[i, part], r["d_s"].at[g, i], r["d_r"].at[g, i], device)
            pending.append((ys.at[i, part], r["d_s"].at[g, i]))

    def home(g):
        total = chip_rows(g, y, rows_in(g))
        for i in range(2):
            wait(yr.at[i, half_rows(g, 1 - i)], r["e_r"].at[g, i])
            wait(yr.at[i, half_rows(g, i)], r["d_r"].at[g, i])
            total = total + yr[i, rows_in(g)].astype(F32)
        to_pieces(expansion(sizes[g]), total.astype(BF16), hs, slots_of(g, TILE))
        group_peers(
            g,
            -1,
            lambda j, p: send(
                hs.at[:, rows_of(j)], ret.at[:, rows_of(s)], r["h_s"].at[g], m_r.at[5], (p, tp)
            ),
        )
        pending.append((group_ref(g), r["h_s"].at[g]))
        if g == home_group:
            ret[:, rows_of(s)] = hs[:, home_slot * TILE : (home_slot + 1) * TILE]

    for copy in weights[tp_n + 1 :]:
        copy.wait()
    stages = (spread_out, pass_on, pass_far, expert, sum_far, sum_near, home)
    todo = {g: list(stages) for g in range(len(groups))}
    for g in c["order"]:
        todo[g].pop(0)(g)

    wait(cr.at[pl.ds(0, tp_n - 1)], m_r.at[4])
    gates = []
    for j in range(2):
        logit = cr[0, j]
        for u in range(1, tp_n):
            logit = logit + cr[u, j]
        gates.append(jax.nn.sigmoid(logit))
    both = gates[0] + gates[1]
    shares = [to_column(gate / both) for gate in gates]
    wait(ret.at[:, pl.ds(0, (n - 1) * TILE)], m_r.at[5])
    mixed = hidden
    for j in range(2):
        parts = [r["q"][j, i] for i in range(3)]
        mixed = mixed + shares[j] * from_pieces(parts, ret, pl.ds(0, n * TILE))
    out[...] = mixed.astype(BF16)

    for ref, sem in pending:
        wait(ref, sem)


DIRECT = {8: ()}
GROUPS = {8: [(1, 7), (2, 6), (3, 5), (0, 4)]}
ORDERS = {8: [0, 1, 0, 2, 0, 1, 3, 0, 2, 1, 0, 1, 3, 1, 2, 2, 0, 2, 3, 3, 1, 2, 0, 3, 1, 2, 3, 3]}


def stepped(count, stages=7):
    return [
        step - lag
        for step in range(count + stages - 1)
        for lag in range(stages)
        if 0 <= step - lag < count
    ]


def body(
    sizes,
    queries,
    keys,
    values,
    log_decay,
    residual,
    out_weight,
    prenorm_multiplier,
    router_weight,
    picked_unit_indices,
    expert_up_weight,
    down_weight,
):
    n, xs, zs, ys = sizes
    half = zs // 2
    groups = GROUPS.get(zs) or [(d, zs - d) for d in range(1, half)] + [(0, half)]
    order = ORDERS.get(zs) or stepped(len(groups))
    heads = log_decay.shape[0]
    c = dict(
        n=n,
        x=xs,
        z=zs,
        y=ys,
        groups=groups,
        order=order,
        direct=DIRECT.get(zs, ()),
        g=len(groups),
        heads=heads,
        t=queries.shape[0],
        a=queries.shape[1],
        w=residual.shape[1],
        f=expert_up_weight.shape[2],
        hd=heads * 128 // n,
    )
    scratch = scratch_of(c)
    vmem, anywhere = pl.BlockSpec(memory_space=pltpu.VMEM), pl.BlockSpec(memory_space=pl.ANY)
    return pl.pallas_call(
        functools.partial(kernel, c, list(scratch)),
        out_shape=jax.ShapeDtypeStruct(residual.shape, BF16),
        in_specs=[vmem] * 7 + [anywhere] * 4,
        out_specs=vmem,
        scratch_shapes=list(scratch.values()),
        compiler_params=pltpu.CompilerParams(
            collective_id=0, has_side_effects=True, vmem_limit_bytes=56 * 1024 * 1024
        ),
    )(
        queries,
        keys,
        values,
        log_decay,
        residual,
        prenorm_multiplier,
        picked_unit_indices.T,
        out_weight,
        router_weight.T,
        expert_up_weight,
        down_weight,
    )


def solution(mesh):
    n = mesh.shape["seq"]
    xs = 4 if n % 4 == 0 and n > 4 else 2
    sizes = (n, xs, n // xs, mesh.shape["tp"] // CORES)
    in_specs = (
        P("seq", "tp"),
        P("seq", "tp"),
        P("seq", "tp"),
        P("tp", "seq"),
        P("seq", "tp"),
        P("tp", None),
        P("tp"),
        P(),
        P("seq", None),
        P("seq", None, "tp"),
        P("seq", "tp", None),
    )
    return jax.shard_map(
        functools.partial(body, sizes),
        mesh=mesh,
        in_specs=in_specs,
        out_specs=P("seq", "tp"),
        check_vma=False,
    )
```

```python
import functools

import jax
import jax.numpy as jnp
from jax import lax
from jax.experimental import pallas as pl
from jax.experimental.pallas import tpu as pltpu
from jax.sharding import PartitionSpec as P

EPSILON = 1e-05
MESH = pl.DeviceIdType.MESH
F32, BF16 = jnp.float32, jnp.bfloat16
HIGHEST = lax.Precision.HIGHEST
CAP = 24
TILE = 16
PIECES = 5
CORES = 2


def mm(a, b):
    return jnp.dot(a, b, preferred_element_type=F32)


def mm_nt(a, b):
    return lax.dot_general(a, b, (((1,), (1,)), ((), ())), preferred_element_type=F32)


def mm_tn(a, b):
    return lax.dot_general(a, b, (((0,), (0,)), ((), ())), preferred_element_type=F32)


def iota(shape, dim):
    return lax.broadcasted_iota(jnp.int32, shape, dim)


def flag(mask):
    return jnp.where(mask, 1.0, 0.0).astype(BF16)


def split2(x):
    high = x.astype(BF16)
    return high, (x - high.astype(F32)).astype(BF16)


def to_column(row):
    n = row.shape[1]
    eye = iota((n, n), 0) == iota((n, n), 1)
    return jnp.sum(jnp.where(eye, row, 0.0), axis=1, keepdims=True)


def to_row(column):
    n = column.shape[0]
    eye = iota((n, n), 0) == iota((n, n), 1)
    return jnp.sum(jnp.where(eye, column, 0.0), axis=0, keepdims=True)


def places(block, slot):
    late = slot >= TILE
    base = block * TILE + slot
    nowhere = jnp.full(base.shape, -1, base.dtype)
    return (
        jnp.where(late, nowhere, base),
        jnp.where(late, base - TILE, nowhere),
        jnp.where(late, base - TILE // 2, nowhere),
    )


def to_pieces(parts, rows, out, where):
    head = mm(parts[0], rows).astype(BF16)
    for i in range(3):
        out[i, where] = head[:, i * 128 : (i + 1) * 128]
    tail = mm(parts[1], rows[:, 0:128]) + mm(parts[2], rows[:, 128:256])
    out[3, where] = tail.astype(BF16)
    out[4, where] = mm(parts[1], rows[:, 256:384]).astype(BF16)


def from_pieces(parts, pieces, where):
    head = jnp.concatenate([pieces[i, where] for i in range(3)], axis=1)
    third, fourth = pieces[3, where], pieces[4, where]
    tail = [mm(parts[1], third), mm(parts[2], third), mm(parts[1], fourth)]
    return mm(parts[0], head) + jnp.concatenate(tail, axis=1)


def send(src, dst, send_sem, recv_sem, device):
    pltpu.make_async_remote_copy(
        src_ref=src,
        dst_ref=dst,
        send_sem=send_sem,
        recv_sem=recv_sem,
        device_id=device,
        device_id_type=MESH,
    ).start()


def wait(ref, sem):
    pltpu.make_async_copy(ref, ref, sem).wait()


def scratch_of(c):
    n, y, g, w, t, hd = c["n"], c["y"], c["g"], c["w"], c["t"], c["hd"]
    tp, f, rows = y * CORES, c["f"], n * CAP
    dma = pltpu.SemaphoreType.DMA
    return dict(
        owv=pltpu.VMEM((tp, c["a"], w), BF16),
        rwv=pltpu.VMEM((n, w), BF16),
        upv=pltpu.VMEM((y, CORES * w, f), BF16),
        dnv=pltpu.VMEM((y, f, CORES * w), BF16),
        ub=pltpu.VMEM((n, hd, 128), BF16),
        ur=pltpu.VMEM((n, hd, 128), BF16),
        ts=pltpu.VMEM((c["heads"], 1, 128), F32),
        tr=pltpu.VMEM((n, 1, 128), F32),
        sb=pltpu.VMEM((n, hd, 128), BF16),
        se=pltpu.VMEM((n, hd, 128), BF16),
        within=pltpu.VMEM((t, c["a"]), F32),
        ps1=pltpu.VMEM((y, t, w), BF16),
        pr1=pltpu.VMEM((y, t, w), BF16),
        ps2=pltpu.VMEM((y, t, w), BF16),
        pr2=pltpu.VMEM((y, t, w), BF16),
        rl1=pltpu.VMEM((2, t // 2, w), BF16),
        sqs=pltpu.VMEM((1, t), F32),
        sqr=pltpu.VMEM((tp, 1, t), F32),
        fs=pltpu.VMEM((n, 1, 128), F32),
        fr=pltpu.VMEM((n, 1, 128), F32),
        cs=pltpu.VMEM((2, 1, t), F32),
        cr=pltpu.VMEM((tp, 2, 1, t), F32),
        pm=pltpu.VMEM((3, n * TILE, t), BF16),
        q=pltpu.VMEM((2, 3, t, n * TILE), BF16),
        dsp=pltpu.VMEM((PIECES, n * TILE, 128), BF16),
        xr=pltpu.VMEM((PIECES, n * TILE, 128), BF16),
        xg=pltpu.VMEM((tp, rows, w), BF16),
        mb=pltpu.VMEM((y, rows, w), F32),
        ps=pltpu.VMEM((y, rows, w), BF16),
        pr=pltpu.VMEM((y, rows, w), BF16),
        ys=pltpu.VMEM((y, rows, w), BF16),
        yr=pltpu.VMEM((y, rows, w), BF16),
        rl=pltpu.VMEM((rows, w), BF16),
        hs=pltpu.VMEM((PIECES, n * TILE, 128), BF16),
        ret=pltpu.VMEM((PIECES, n * TILE, 128), BF16),
        w_ow=dma((tp,)),
        w_up=dma((y,)),
        w_dn=dma((y,)),
        w_rw=dma((1,)),
        m_s=dma((8,)),
        m_r=dma((8,)),
        p1_s=dma((y,)),
        p1_r=dma((y,)),
        p2_s=dma((y,)),
        p2_r=dma((y,)),
        p3_s=dma((2,)),
        p3_r=dma((2,)),
        l1_s=dma((2,)),
        l1_r=dma((2,)),
        x_s=dma((g,)),
        x_r=dma((g,)),
        a_s=dma((g, y)),
        a_r=dma((g, y)),
        b_s=dma((g, y)),
        b_r=dma((g, y)),
        c_s=dma((g, y)),
        c_r=dma((g, y)),
        d_s=dma((g, y)),
        d_r=dma((g, y)),
        e_s=dma((g, 2)),
        e_r=dma((g, 2)),
        f_s=dma((g, 2)),
        f_r=dma((g, 2)),
        l_s=dma((g, 2)),
        l_r=dma((g, 2)),
        h_s=dma((g,)),
    )


def kernel(c, names, *refs):
    (q, k, v, ld, res, mult, idst, ow, rw, up, dn, out) = refs[:12]
    r = dict(zip(names, refs[12:]))
    n, xs, zs, ys_n, groups = c["n"], c["x"], c["z"], c["y"], c["groups"]
    heads, t, w, hd, tp_n = c["heads"], c["t"], c["w"], c["hd"], c["y"] * CORES
    starts = [xs * sum(len(steps) for steps in groups[:g]) for g in range(len(groups))]
    sizes = [xs * len(steps) for steps in groups]
    s, tp = lax.axis_index("seq"), lax.axis_index("tp")
    z, x = s // xs, lax.rem(s, xs)
    y, core = tp // CORES, lax.rem(tp, CORES)
    partner = (s, y * CORES + 1 - core)
    ahead, behind, opposite = (lax.rem(y + d, ys_n) for d in (1, 3, 2))
    sides = ((ahead, (s, ahead * CORES + core)), (behind, (s, behind * CORES + core)))
    m_s, m_r = r["m_s"], r["m_r"]

    def seq_peers(body):
        def step(i, carry):
            distance = (n - i + 1) // 2
            body(lax.rem(s + jnp.where(lax.rem(i, 2) == 1, distance, n - distance), n))
            return carry

        lax.fori_loop(1, n, step, 0)

    def tp_peers(body):
        def step(i, carry):
            body(lax.rem(tp + i, tp_n))
            return carry

        lax.fori_loop(1, tp_n, step, 0)

    pending, last_sent = [], []
    barrier = pltpu.get_barrier_semaphore()
    seq_peers(
        lambda p: pl.semaphore_signal(barrier, inc=1, device_id=(p, tp), device_id_type=MESH)
    )
    tp_peers(lambda p: pl.semaphore_signal(barrier, inc=1, device_id=(s, p), device_id_type=MESH))

    weights = []
    for u in range(tp_n):
        weights.append(
            pltpu.make_async_copy(ow.at[:, pl.ds(u * w, w)], r["owv"].at[u], r["w_ow"].at[u])
        )
    weights.append(
        pltpu.make_async_copy(
            rw.at[:, pl.ds(pl.multiple_of(tp * w, w), w)], r["rwv"], r["w_rw"].at[0]
        )
    )
    for i in range(ys_n):
        part = pl.ds(i * CORES * w, CORES * w)
        weights.append(
            pltpu.make_async_copy(up.at[0, part, :], r["upv"].at[i], r["w_up"].at[i])
        )
    for i in range(ys_n):
        part = pl.ds(i * CORES * w, CORES * w)
        weights.append(
            pltpu.make_async_copy(dn.at[0, :, part], r["dnv"].at[i], r["w_dn"].at[i])
        )
    for copy in weights:
        copy.start()

    logs = ld[...]
    upper = jnp.where(iota((t, t), 0) <= iota((t, t), 1), 1.0, 0.0)
    lower = jnp.where(iota((t, t), 0) >= iota((t, t), 1), 1.0, 0.0)
    c_row = jnp.dot(logs, upper, precision=HIGHEST, preferred_element_type=F32)
    c_col = lax.dot_general(
        lower, logs, (((1,), (1,)), ((), ())), precision=HIGHEST, preferred_element_type=F32
    )
    per_head = 128 // hd
    for h in range(heads):
        head = pl.ds(h * 128, 128)
        total = c_row[h : h + 1, t - 1 : t]
        r["ts"][h] = jnp.broadcast_to(total, (1, 128))
        weighted = k[:, head].astype(F32) * jnp.exp(total - c_col[:, h : h + 1])
        high, low = split2(weighted)
        product = (mm_tn(high, v[:, head]) + mm_tn(low, v[:, head])).astype(BF16)
        for i in range(per_head):
            r["ub"][h * per_head + i] = product[i * hd : (i + 1) * hd]

    pl.semaphore_wait(barrier, n - 1 + tp_n - 1)

    ub, ur, ts, tr, sb, se = (r[name] for name in ("ub", "ur", "ts", "tr", "sb", "se"))
    seq_peers(lambda p: send(ts.at[p // per_head], tr.at[s], m_s.at[0], m_r.at[0], (p, tp)))
    seq_peers(lambda p: send(ub.at[p], ur.at[s], m_s.at[1], m_r.at[1], (p, tp)))
    pending.append((tr.at[pl.ds(0, n - 1)], m_s.at[0]))
    pending.append((ur.at[pl.ds(0, n - 1)], m_s.at[1]))
    tr[s] = ts[s // per_head]
    ur[s] = ub[s]

    ids_r = idst[...]
    first, second = (to_column(ids_r[j : j + 1, :].astype(F32)) for j in range(2))
    picks = (first, second)
    names_lane = iota((t, n), 1).astype(F32)
    slots_c = []
    before = flag(iota((t, t), 1) < iota((t, t), 0))
    counts = mm(before, flag((first == names_lane) | (second == names_lane)))
    for j, pick in enumerate(picks):
        slot = jnp.sum(jnp.where(pick == names_lane, counts, 0.0), axis=1, keepdims=True)
        slots_c.append(slot)
        for i, target in enumerate(places(pick, slot)):
            r["q"][j, i] = flag(iota((t, n * TILE), 1).astype(F32) == target)
    first, second = ids_r[0:1, :], ids_r[1:2, :]
    names_sub = iota((n, t), 0)
    after = flag(iota((t, t), 0) < iota((t, t), 1))
    counts = mm(flag((first == names_sub) | (second == names_sub)), after)
    targets = []
    for pick in (first, second):
        slot = jnp.sum(jnp.where(pick == names_sub, counts, 0.0), axis=0, keepdims=True)
        targets.append(places(pick.astype(F32), slot))
    place = iota((n * TILE, t), 0).astype(F32)
    for i in range(3):
        r["pm"][i] = flag((place == targets[0][i]) | (place == targets[1][i]))

    causal = iota((t, t), 0) >= iota((t, t), 1)
    for h in range(heads):
        head = pl.ds(h * 128, 128)
        scores = mm_nt(q[:, head], k[:, head])
        gap = jnp.where(causal, c_col[:, h : h + 1] - c_row[h : h + 1, :], 0.0)
        intra = jnp.where(causal, scores * jnp.exp(gap), 0.0).astype(BF16)
        r["within"][:, head] = mm(intra, v[:, head])

    wait(tr.at[pl.ds(0, n - 1)], m_r.at[0])
    wait(ur.at[pl.ds(0, n - 1)], m_r.at[1])

    def scan(b, state):
        sb[b] = state.astype(BF16)
        return jnp.exp(tr[b]) * state + ur[b].astype(F32)

    lax.fori_loop(0, n, scan, jnp.zeros((hd, 128), F32))
    seq_peers(lambda p: send(sb.at[p], se.at[s], m_s.at[2], m_r.at[2], (p, tp)))
    pending.append((se.at[pl.ds(0, n - 1)], m_s.at[2]))
    se[s] = sb[s]
    wait(se.at[pl.ds(0, n - 1)], m_r.at[2])

    attended = []
    for h in range(heads):
        head = pl.ds(h * 128, 128)
        state = se[h * per_head : (h + 1) * per_head].reshape(128, 128)
        head_out = r["within"][:, head] + mm(q[:, head], state) * jnp.exp(c_col[:, h : h + 1])
        mean = jnp.mean(head_out * head_out, axis=1, keepdims=True)
        attended.append((head_out * lax.rsqrt(mean + EPSILON)).astype(BF16))
    attention = jnp.concatenate(attended, axis=1)

    ps1, pr1, ps2, pr2 = (r[name] for name in ("ps1", "pr1", "ps2", "pr2"))
    for copy in weights[: tp_n + 1]:
        copy.wait()
    for to in (opposite, ahead, behind, y):
        ps1[to] = mm(attention, r["owv"][to * CORES + 1 - core]).astype(BF16)
        send(ps1.at[to], pr1.at[to], r["p1_s"].at[to], r["p1_r"].at[to], partner)
        pending.append((ps1.at[to], r["p1_s"].at[to]))

    def chip_sum(to):
        mine = mm(attention, r["owv"][to * CORES + core])
        wait(pr1.at[to], r["p1_r"].at[to])
        return mine + pr1[to].astype(F32)

    rl1 = r["rl1"]
    halves = (pl.ds(0, t // 2), pl.ds(t // 2, t // 2))
    ps2[2] = chip_sum(opposite).astype(BF16)
    for i, (_, device) in enumerate(sides):
        send(ps2.at[2, halves[i]], rl1.at[i], r["l1_s"].at[i], r["l1_r"].at[i], device)
        pending.append((rl1.at[i], r["l1_s"].at[i]))
    with_relay = []
    for i, (to, device) in enumerate(sides):
        mine = chip_sum(to)
        ps2[i, halves[1 - i]] = mine[(1 - i) * (t // 2) : (2 - i) * (t // 2)].astype(BF16)
        piece = (i, halves[1 - i])
        send(ps2.at[piece], pr2.at[piece], r["p3_s"].at[i], r["p3_r"].at[i], device)
        pending.append((ps2.at[piece], r["p3_s"].at[i]))
        with_relay.append(mine[i * (t // 2) : (i + 1) * (t // 2)])
    for i, (_, device) in enumerate(sides):
        wait(rl1.at[i], r["l1_r"].at[i])
        piece = (i, halves[i])
        ps2[piece] = (with_relay[i] + rl1[i].astype(F32)).astype(BF16)
        send(ps2.at[piece], pr2.at[piece], r["p2_s"].at[i], r["p2_r"].at[i], device)
        pending.append((ps2.at[piece], r["p2_s"].at[i]))
    hidden = res[...].astype(F32) + chip_sum(y)
    for i in range(2):
        wait(pr2.at[i, halves[1 - i]], r["p3_r"].at[i])
        wait(pr2.at[i, halves[i]], r["p2_r"].at[i])
        hidden = hidden + pr2[i].astype(F32)

    dsp, xr, ret = r["dsp"], r["xr"], r["ret"]
    scaled = (hidden * mult[...][None, :]).astype(BF16)
    to_pieces([r["pm"][i] for i in range(3)], scaled, dsp, pl.ds(0, n * TILE))

    def rows_of(index):
        return pl.ds(pl.multiple_of(index * TILE, TILE), TILE)

    home_group = [g for g, steps in enumerate(groups) if steps[0] == 0][0]
    home_slot = starts[home_group]

    def group_peers(g, sign, body):
        first = 0 if g != home_group else 1

        def step(i, carry):
            j = sizes[g] - 1 + first - i
            dz = groups[g][0]
            for chip in range(1, len(groups[g])):
                dz = jnp.where(j < chip * xs, dz, groups[g][chip])
            dx = lax.rem(j, xs)
            pz = lax.rem(z + zs + sign * dz, zs)
            px = lax.rem(x + xs + sign * dx, xs)
            body(starts[g] + j, pz * xs + px)
            return carry

        lax.fori_loop(first, sizes[g], step, 0)

    for g in range(len(groups)):
        group_peers(
            g,
            1,
            lambda j, p, g=g: send(
                dsp.at[:, rows_of(p)], xr.at[:, rows_of(j)], r["x_s"].at[g], r["x_r"].at[g], (p, tp)
            ),
        )
    def group_ref(g):
        skip = 1 if g == home_group else 0
        return xr.at[:, pl.ds((starts[g] + skip) * TILE, (sizes[g] - skip) * TILE)]

    for g in range(len(groups)):
        pending.append((group_ref(g), r["x_s"].at[g]))
    xr[:, home_slot * TILE : (home_slot + 1) * TILE] = dsp[:, rows_of(s)]

    sqs, sqr = r["sqs"], r["sqr"]
    high, low = split2(hidden * hidden)
    ones = jnp.ones((8, w), BF16)
    sqs[...] = (mm_nt(ones, high) + mm_nt(ones, low))[0:1]
    tp_peers(lambda p: send(sqs, sqr.at[tp], m_s.at[3], m_r.at[3], (s, p)))
    pending.append((sqr.at[pl.ds(0, tp_n - 1)], m_s.at[3]))
    sqr[tp] = sqs[...]
    partial_logits = mm_nt(scaled, r["rwv"][...])
    wait(sqr.at[pl.ds(0, tp_n - 1)], m_r.at[3])
    square_sum = sqr[0]
    for u in range(1, tp_n):
        square_sum = square_sum + sqr[u]
    inverse = to_column(lax.rsqrt(square_sum / (w * tp_n) + EPSILON))
    factors = jnp.zeros((n, 128), F32)
    lane = iota((t, 128), 1).astype(F32)
    for pick, slot in zip(picks, slots_c):
        chosen = flag(pick == names_lane)
        rest = jnp.where(slot == lane, inverse, 0.0)
        for _ in range(3):
            piece = rest.astype(BF16)
            rest = rest - piece.astype(F32)
            factors = factors + mm_tn(chosen, piece)
    fs, fr = r["fs"], r["fr"]
    for i in range(n):
        fs[i] = factors[i : i + 1]
    for g in range(len(groups)):
        group_peers(
            g,
            1,
            lambda j, p, g=g: send(
                fs.at[p], fr.at[j], m_s.at[6], m_r.at[6], (p, tp)
            ),
        )
    pending.append((fr.at[pl.ds(0, n - 1)], m_s.at[6]))
    fr[home_slot] = fs[s]

    cs, cr = r["cs"], r["cr"]
    logits = partial_logits * inverse
    for j in range(2):
        chosen = jnp.where(picks[j] == names_lane, logits, 0.0)
        cs[j] = to_row(jnp.sum(chosen, axis=1, keepdims=True))
    tp_peers(lambda p: send(cs, cr.at[tp], m_s.at[4], m_r.at[4], (s, p)))
    pending.append((cr.at[pl.ds(0, tp_n - 1)], m_s.at[4]))
    cr[tp] = cs[...]

    xg, mb, ps, pr = (r[name] for name in ("xg", "mb", "ps", "pr"))
    ys, yr, rl, hs = (r[name] for name in ("ys", "yr", "rl", "hs"))

    def compaction(count):
        row, lane = iota((count * CAP, count * TILE), 0), iota((count * CAP, count * TILE), 1)
        block = (row * 2731) >> 16
        return [flag(lane == place) for place in places(block, row - block * CAP)]

    def expansion(count):
        row, lane = iota((count * TILE, count * CAP), 0), iota((count * TILE, count * CAP), 1)
        block = (lane * 2731) >> 16
        return [flag(row == place) for place in places(block, lane - block * CAP)]

    def slots_of(g, unit):
        return pl.ds(starts[g] * unit, sizes[g] * unit)

    def rows_in(g):
        return slots_of(g, CAP)

    def half_rows(g, i):
        return pl.ds(starts[g] * CAP + i * sizes[g] * CAP // 2, sizes[g] * CAP // 2)

    origins = (behind, ahead)

    def spread_out(g):
        wait(group_ref(g), r["x_r"].at[g])
        packed = from_pieces(compaction(sizes[g]), xr, slots_of(g, TILE)).astype(BF16)
        xg[tp, rows_in(g)] = packed
        piece = xg.at[tp, rows_in(g)]
        for i, (_, device) in enumerate(sides):
            send(piece, piece, r["a_s"].at[g, i], r["a_r"].at[g, i], device)
            pending.append((piece, r["a_s"].at[g, i]))
        if g in c["direct"]:
            across = (s, opposite * CORES + core)
            send(piece, piece, r["a_s"].at[g, 2], r["a_r"].at[g, 2], across)
            pending.append((piece, r["a_s"].at[g, 2]))
        send(piece, piece, r["b_s"].at[g, y], r["b_r"].at[g, y], partner)
        pending.append((piece, r["b_s"].at[g, y]))

    def pass_over(g, block):
        piece = xg.at[block * CORES + core, rows_in(g)]
        send(piece, piece, r["b_s"].at[g, block], r["b_r"].at[g, block], partner)
        pending.append((piece, r["b_s"].at[g, block]))

    def pass_on(g):
        for i, (_, device) in enumerate(sides):
            wait(xg.at[origins[i] * CORES + core, rows_in(g)], r["a_r"].at[g, i])
            if g not in c["direct"]:
                piece = xg.at[origins[i] * CORES + core, half_rows(g, i)]
                send(piece, piece, r["f_s"].at[g, i], r["f_r"].at[g, i], device)
                pending.append((piece, r["f_s"].at[g, i]))
            pass_over(g, origins[i])

    def pass_far(g):
        if g in c["direct"]:
            wait(xg.at[opposite * CORES + core, rows_in(g)], r["a_r"].at[g, 2])
        else:
            for i in range(2):
                wait(xg.at[opposite * CORES + core, half_rows(g, i)], r["f_r"].at[g, i])
        pass_over(g, opposite)

    waited = []

    def expert(g):
        for i in range(ys_n):
            wait(xg.at[i * CORES + 1 - core, rows_in(g)], r["b_r"].at[g, i])
        total = jnp.zeros((sizes[g] * CAP, c["f"]), F32)
        for i in range(ys_n):
            both = [xg[i * CORES + side, rows_in(g)] for side in range(CORES)]
            total = total + mm(jnp.concatenate(both, axis=1), r["upv"][i])
        if not waited:
            wait(fr.at[pl.ds(0, n - 1)], m_r.at[6])
            waited.append(g)
        mine = range(starts[g], starts[g] + sizes[g])
        spots = [jnp.broadcast_to(fr[j], (CAP, 128)) for j in mine]
        spots = jnp.concatenate(spots, axis=0)
        spot_row, spot_lane = iota((sizes[g] * CAP, 128), 0), iota((sizes[g] * CAP, 128), 1)
        spot_row = spot_row - ((spot_row * 2731) >> 16) * CAP
        total = total * jnp.sum(jnp.where(spot_lane == spot_row, spots, 0.0), axis=1, keepdims=True)
        hidden_rows = (total / (1.0 + jnp.exp(-total))).astype(BF16)
        for i in range(ys_n):
            part = mm(hidden_rows, r["dnv"][i])
            left, right = part[:, :w], part[:, w:]
            mb[i, rows_in(g)] = jnp.where(core == 0, left, right)
            ps[i, rows_in(g)] = jnp.where(core == 0, right, left).astype(BF16)
            piece = (i, rows_in(g))
            send(ps.at[piece], pr.at[piece], r["c_s"].at[g, i], r["c_r"].at[g, i], partner)
            pending.append((ps.at[piece], r["c_s"].at[g, i]))

    def chip_rows(g, to, part):
        return mb[to, part] + pr[to, part].astype(F32)

    def sum_far(g):
        for i in range(ys_n):
            wait(pr.at[i, rows_in(g)], r["c_r"].at[g, i])
        for i, (_, device) in enumerate(sides):
            part = half_rows(g, i)
            ys[2, part] = chip_rows(g, opposite, part).astype(BF16)
            send(ys.at[2, part], rl.at[part], r["l_s"].at[g, i], r["l_r"].at[g, i], device)
            pending.append((ys.at[2, part], r["l_s"].at[g, i]))
        for i, (to, device) in enumerate(sides):
            part = half_rows(g, 1 - i)
            ys[i, part] = chip_rows(g, to, part).astype(BF16)
            send(ys.at[i, part], yr.at[i, part], r["e_s"].at[g, i], r["e_r"].at[g, i], device)
            pending.append((ys.at[i, part], r["e_s"].at[g, i]))

    def sum_near(g):
        for i, (to, device) in enumerate(sides):
            part = half_rows(g, i)
            wait(rl.at[part], r["l_r"].at[g, i])
            ys[i, part] = (chip_rows(g, to, part) + rl[part].astype(F32)).astype(BF16)
            send(ys.at[i, part], yr.at[i, part], r["d_s"].at[g, i], r["d_r"].at[g, i], device)
            pending.append((ys.at[i, part], r["d_s"].at[g, i]))

    def home(g):
        total = chip_rows(g, y, rows_in(g))
        for i in range(2):
            wait(yr.at[i, half_rows(g, 1 - i)], r["e_r"].at[g, i])
            wait(yr.at[i, half_rows(g, i)], r["d_r"].at[g, i])
            total = total + yr[i, rows_in(g)].astype(F32)
        to_pieces(expansion(sizes[g]), total.astype(BF16), hs, slots_of(g, TILE))
        group_peers(
            g,
            -1,
            lambda j, p: send(
                hs.at[:, rows_of(j)], ret.at[:, rows_of(s)], r["h_s"].at[g], m_r.at[5], (p, tp)
            ),
        )
        last_sent.append((group_ref(g), r["h_s"].at[g]))
        if g == home_group:
            ret[:, rows_of(s)] = hs[:, home_slot * TILE : (home_slot + 1) * TILE]

    for copy in weights[tp_n + 1 :]:
        copy.wait()
    stages = (spread_out, pass_on, pass_far, expert, sum_far, sum_near, home)
    todo = {g: list(stages) for g in range(len(groups))}
    for g in c["order"]:
        todo[g].pop(0)(g)

    wait(cr.at[pl.ds(0, tp_n - 1)], m_r.at[4])
    gates = []
    for j in range(2):
        logit = cr[0, j]
        for u in range(1, tp_n):
            logit = logit + cr[u, j]
        gates.append(jax.nn.sigmoid(logit))
    both = gates[0] + gates[1]
    shares = [to_column(gate / both) for gate in gates]
    for ref, sem in pending:
        wait(ref, sem)
    wait(ret.at[:, pl.ds(0, (n - 1) * TILE)], m_r.at[5])
    mixed = hidden
    for j in range(2):
        parts = [r["q"][j, i] for i in range(3)]
        mixed = mixed + shares[j] * from_pieces(parts, ret, pl.ds(0, n * TILE))
    out[...] = mixed.astype(BF16)

    for ref, sem in last_sent:
        wait(ref, sem)


DIRECT = {8: ()}
GROUPS = {8: [(1, 7), (2, 6), (3, 5), (0, 4)]}
ORDERS = {8: [0, 1, 0, 2, 0, 1, 3, 0, 2, 1, 0, 1, 3, 1, 2, 2, 0, 2, 3, 3, 1, 2, 0, 3, 1, 2, 3, 3]}


def stepped(count, stages=7):
    return [
        step - lag
        for step in range(count + stages - 1)
        for lag in range(stages)
        if 0 <= step - lag < count
    ]


def body(
    sizes,
    queries,
    keys,
    values,
    log_decay,
    residual,
    out_weight,
    prenorm_multiplier,
    router_weight,
    picked_unit_indices,
    expert_up_weight,
    down_weight,
):
    n, xs, zs, ys = sizes
    half = zs // 2
    groups = GROUPS.get(zs) or [(d, zs - d) for d in range(1, half)] + [(0, half)]
    order = ORDERS.get(zs) or stepped(len(groups))
    heads = log_decay.shape[0]
    c = dict(
        n=n,
        x=xs,
        z=zs,
        y=ys,
        groups=groups,
        order=order,
        direct=DIRECT.get(zs, ()),
        g=len(groups),
        heads=heads,
        t=queries.shape[0],
        a=queries.shape[1],
        w=residual.shape[1],
        f=expert_up_weight.shape[2],
        hd=heads * 128 // n,
    )
    scratch = scratch_of(c)
    vmem, anywhere = pl.BlockSpec(memory_space=pltpu.VMEM), pl.BlockSpec(memory_space=pl.ANY)
    return pl.pallas_call(
        functools.partial(kernel, c, list(scratch)),
        out_shape=jax.ShapeDtypeStruct(residual.shape, BF16),
        in_specs=[vmem] * 7 + [anywhere] * 4,
        out_specs=vmem,
        scratch_shapes=list(scratch.values()),
        compiler_params=pltpu.CompilerParams(
            collective_id=0, has_side_effects=True, vmem_limit_bytes=56 * 1024 * 1024
        ),
    )(
        queries,
        keys,
        values,
        log_decay,
        residual,
        prenorm_multiplier,
        picked_unit_indices.T,
        out_weight,
        router_weight.T,
        expert_up_weight,
        down_weight,
    )


def solution(mesh):
    n = mesh.shape["seq"]
    xs = 4 if n % 4 == 0 and n > 4 else 2
    sizes = (n, xs, n // xs, mesh.shape["tp"] // CORES)
    in_specs = (
        P("seq", "tp"),
        P("seq", "tp"),
        P("seq", "tp"),
        P("tp", "seq"),
        P("seq", "tp"),
        P("tp", None),
        P("tp"),
        P(),
        P("seq", None),
        P("seq", None, "tp"),
        P("seq", "tp", None),
    )
    return jax.shard_map(
        functools.partial(body, sizes),
        mesh=mesh,
        in_specs=in_specs,
        out_specs=P("seq", "tp"),
        check_vma=False,
    )
```

```python
import functools

import jax
import jax.numpy as jnp
from jax import lax
from jax.experimental import pallas as pl
from jax.experimental.pallas import tpu as pltpu
from jax.sharding import PartitionSpec as P

EPSILON = 1e-05
MESH = pl.DeviceIdType.MESH
F32, BF16 = jnp.float32, jnp.bfloat16
HIGHEST = lax.Precision.HIGHEST
CAP = 24
TILE = 16
PIECES = 5
CORES = 2


def mm(a, b):
    return jnp.dot(a, b, preferred_element_type=F32)


def mm_nt(a, b):
    return lax.dot_general(a, b, (((1,), (1,)), ((), ())), preferred_element_type=F32)


def mm_tn(a, b):
    return lax.dot_general(a, b, (((0,), (0,)), ((), ())), preferred_element_type=F32)


def iota(shape, dim):
    return lax.broadcasted_iota(jnp.int32, shape, dim)


def flag(mask):
    return jnp.where(mask, 1.0, 0.0).astype(BF16)


def split2(x):
    high = x.astype(BF16)
    return high, (x - high.astype(F32)).astype(BF16)


def to_column(row):
    n = row.shape[1]
    eye = iota((n, n), 0) == iota((n, n), 1)
    return jnp.sum(jnp.where(eye, row, 0.0), axis=1, keepdims=True)


def to_row(column):
    n = column.shape[0]
    eye = iota((n, n), 0) == iota((n, n), 1)
    return jnp.sum(jnp.where(eye, column, 0.0), axis=0, keepdims=True)


def places(block, slot):
    late = slot >= TILE
    base = block * TILE + slot
    nowhere = jnp.full(base.shape, -1, base.dtype)
    return (
        jnp.where(late, nowhere, base),
        jnp.where(late, base - TILE, nowhere),
        jnp.where(late, base - TILE // 2, nowhere),
    )


def to_pieces(parts, rows, out, where):
    head = mm(parts[0], rows).astype(BF16)
    for i in range(3):
        out[i, where] = head[:, i * 128 : (i + 1) * 128]
    tail = mm(parts[1], rows[:, 0:128]) + mm(parts[2], rows[:, 128:256])
    out[3, where] = tail.astype(BF16)
    out[4, where] = mm(parts[1], rows[:, 256:384]).astype(BF16)


def from_pieces(parts, pieces, where):
    head = jnp.concatenate([pieces[i, where] for i in range(3)], axis=1)
    third, fourth = pieces[3, where], pieces[4, where]
    tail = [mm(parts[1], third), mm(parts[2], third), mm(parts[1], fourth)]
    return mm(parts[0], head) + jnp.concatenate(tail, axis=1)


def send(src, dst, send_sem, recv_sem, device):
    pltpu.make_async_remote_copy(
        src_ref=src,
        dst_ref=dst,
        send_sem=send_sem,
        recv_sem=recv_sem,
        device_id=device,
        device_id_type=MESH,
    ).start()


def wait(ref, sem):
    pltpu.make_async_copy(ref, ref, sem).wait()


def scratch_of(c):
    n, y, g, w, t, hd = c["n"], c["y"], c["g"], c["w"], c["t"], c["hd"]
    tp, f, rows = y * CORES, c["f"], n * CAP
    dma = pltpu.SemaphoreType.DMA
    return dict(
        owv=pltpu.VMEM((tp, c["a"], w), BF16),
        rwv=pltpu.VMEM((n, w), BF16),
        upv=pltpu.VMEM((y, CORES * w, f), BF16),
        dnv=pltpu.VMEM((y, f, CORES * w), BF16),
        ub=pltpu.VMEM((n, hd, 128), BF16),
        ur=pltpu.VMEM((n, hd, 128), BF16),
        ts=pltpu.VMEM((c["heads"], 1, 128), F32),
        tr=pltpu.VMEM((n, 1, 128), F32),
        sb=pltpu.VMEM((n, hd, 128), BF16),
        se=pltpu.VMEM((n, hd, 128), BF16),
        within=pltpu.VMEM((t, c["a"]), F32),
        ps1=pltpu.VMEM((y, t, w), BF16),
        pr1=pltpu.VMEM((y, t, w), BF16),
        ps2=pltpu.VMEM((y, t, w), BF16),
        pr2=pltpu.VMEM((y, t, w), BF16),
        rl1=pltpu.VMEM((2, t // 2, w), BF16),
        sqs=pltpu.VMEM((1, t), F32),
        sqr=pltpu.VMEM((tp, 1, t), F32),
        fs=pltpu.VMEM((n, 1, 128), F32),
        fr=pltpu.VMEM((n, 1, 128), F32),
        cs=pltpu.VMEM((2, 1, t), F32),
        cr=pltpu.VMEM((tp, 2, 1, t), F32),
        pm=pltpu.VMEM((3, n * TILE, t), BF16),
        q=pltpu.VMEM((2, 3, t, n * TILE), BF16),
        dsp=pltpu.VMEM((PIECES, n * TILE, 128), BF16),
        xr=pltpu.VMEM((PIECES, n * TILE, 128), BF16),
        xg=pltpu.VMEM((tp, rows, w), BF16),
        mb=pltpu.VMEM((y, rows, w), F32),
        ps=pltpu.VMEM((y, rows, w), BF16),
        pr=pltpu.VMEM((y, rows, w), BF16),
        ys=pltpu.VMEM((y, rows, w), BF16),
        yr=pltpu.VMEM((y, rows, w), BF16),
        rl=pltpu.VMEM((rows, w), BF16),
        hs=pltpu.VMEM((PIECES, n * TILE, 128), BF16),
        ret=pltpu.VMEM((PIECES, n * TILE, 128), BF16),
        w_ow=dma((tp,)),
        w_up=dma((y,)),
        w_dn=dma((y,)),
        w_rw=dma((1,)),
        m_s=dma((8,)),
        m_r=dma((8,)),
        p1_s=dma((y,)),
        p1_r=dma((y,)),
        p2_s=dma((y,)),
        p2_r=dma((y,)),
        p3_s=dma((2,)),
        p3_r=dma((2,)),
        l1_s=dma((2,)),
        l1_r=dma((2,)),
        x_s=dma((g,)),
        x_r=dma((g,)),
        a_s=dma((g, y)),
        a_r=dma((g, y)),
        b_s=dma((g, y)),
        b_r=dma((g, y)),
        c_s=dma((g, y)),
        c_r=dma((g, y)),
        d_s=dma((g, y)),
        d_r=dma((g, y)),
        e_s=dma((g, 2)),
        e_r=dma((g, 2)),
        f_s=dma((g, 2)),
        f_r=dma((g, 2)),
        l_s=dma((g, 2)),
        l_r=dma((g, 2)),
        h_s=dma((g,)),
    )


def kernel(c, names, *refs):
    (q, k, v, ld, res, mult, idst, ow, rw, up, dn, out) = refs[:12]
    r = dict(zip(names, refs[12:]))
    n, xs, zs, ys_n, groups = c["n"], c["x"], c["z"], c["y"], c["groups"]
    heads, t, w, hd, tp_n = c["heads"], c["t"], c["w"], c["hd"], c["y"] * CORES
    starts = [xs * sum(len(steps) for steps in groups[:g]) for g in range(len(groups))]
    sizes = [xs * len(steps) for steps in groups]
    s, tp = lax.axis_index("seq"), lax.axis_index("tp")
    z, x = s // xs, lax.rem(s, xs)
    y, core = tp // CORES, lax.rem(tp, CORES)
    partner = (s, y * CORES + 1 - core)
    ahead, behind, opposite = (lax.rem(y + d, ys_n) for d in (1, 3, 2))
    sides = ((ahead, (s, ahead * CORES + core)), (behind, (s, behind * CORES + core)))
    m_s, m_r = r["m_s"], r["m_r"]

    def seq_peers(body):
        def step(i, carry):
            distance = (n - i + 1) // 2
            body(lax.rem(s + jnp.where(lax.rem(i, 2) == 1, distance, n - distance), n))
            return carry

        lax.fori_loop(1, n, step, 0)

    def tp_peers(body):
        def step(i, carry):
            body(lax.rem(tp + i, tp_n))
            return carry

        lax.fori_loop(1, tp_n, step, 0)

    pending, last_sent = [], []
    barrier = pltpu.get_barrier_semaphore()
    seq_peers(
        lambda p: pl.semaphore_signal(barrier, inc=1, device_id=(p, tp), device_id_type=MESH)
    )
    tp_peers(lambda p: pl.semaphore_signal(barrier, inc=1, device_id=(s, p), device_id_type=MESH))

    weights = []
    for u in range(tp_n):
        weights.append(
            pltpu.make_async_copy(ow.at[:, pl.ds(u * w, w)], r["owv"].at[u], r["w_ow"].at[u])
        )
    weights.append(
        pltpu.make_async_copy(
            rw.at[:, pl.ds(pl.multiple_of(tp * w, w), w)], r["rwv"], r["w_rw"].at[0]
        )
    )
    for i in range(ys_n):
        part = pl.ds(i * CORES * w, CORES * w)
        weights.append(
            pltpu.make_async_copy(up.at[0, part, :], r["upv"].at[i], r["w_up"].at[i])
        )
    for i in range(ys_n):
        part = pl.ds(i * CORES * w, CORES * w)
        weights.append(
            pltpu.make_async_copy(dn.at[0, :, part], r["dnv"].at[i], r["w_dn"].at[i])
        )
    for copy in weights:
        copy.start()

    logs = ld[...]
    upper = jnp.where(iota((t, t), 0) <= iota((t, t), 1), 1.0, 0.0)
    lower = jnp.where(iota((t, t), 0) >= iota((t, t), 1), 1.0, 0.0)
    c_row = jnp.dot(logs, upper, precision=HIGHEST, preferred_element_type=F32)
    c_col = lax.dot_general(
        lower, logs, (((1,), (1,)), ((), ())), precision=HIGHEST, preferred_element_type=F32
    )
    per_head = 128 // hd
    for h in range(heads):
        head = pl.ds(h * 128, 128)
        total = c_row[h : h + 1, t - 1 : t]
        r["ts"][h] = jnp.broadcast_to(total, (1, 128))
        weighted = k[:, head].astype(F32) * jnp.exp(total - c_col[:, h : h + 1])
        high, low = split2(weighted)
        product = (mm_tn(high, v[:, head]) + mm_tn(low, v[:, head])).astype(BF16)
        for i in range(per_head):
            r["ub"][h * per_head + i] = product[i * hd : (i + 1) * hd]

    pl.semaphore_wait(barrier, n - 1 + tp_n - 1)

    ub, ur, ts, tr, sb, se = (r[name] for name in ("ub", "ur", "ts", "tr", "sb", "se"))
    seq_peers(lambda p: send(ts.at[p // per_head], tr.at[s], m_s.at[0], m_r.at[0], (p, tp)))
    seq_peers(lambda p: send(ub.at[p], ur.at[s], m_s.at[1], m_r.at[1], (p, tp)))
    pending.append((tr.at[pl.ds(0, n - 1)], m_s.at[0]))
    pending.append((ur.at[pl.ds(0, n - 1)], m_s.at[1]))
    tr[s] = ts[s // per_head]
    ur[s] = ub[s]

    ids_r = idst[...]
    first, second = (to_column(ids_r[j : j + 1, :].astype(F32)) for j in range(2))
    picks = (first, second)
    names_lane = iota((t, n), 1).astype(F32)
    slots_c = []
    before = flag(iota((t, t), 1) < iota((t, t), 0))
    counts = mm(before, flag((first == names_lane) | (second == names_lane)))
    for j, pick in enumerate(picks):
        slot = jnp.sum(jnp.where(pick == names_lane, counts, 0.0), axis=1, keepdims=True)
        slots_c.append(slot)
        for i, target in enumerate(places(pick, slot)):
            r["q"][j, i] = flag(iota((t, n * TILE), 1).astype(F32) == target)
    first, second = ids_r[0:1, :], ids_r[1:2, :]
    names_sub = iota((n, t), 0)
    after = flag(iota((t, t), 0) < iota((t, t), 1))
    counts = mm(flag((first == names_sub) | (second == names_sub)), after)
    targets = []
    for pick in (first, second):
        slot = jnp.sum(jnp.where(pick == names_sub, counts, 0.0), axis=0, keepdims=True)
        targets.append(places(pick.astype(F32), slot))
    place = iota((n * TILE, t), 0).astype(F32)
    for i in range(3):
        r["pm"][i] = flag((place == targets[0][i]) | (place == targets[1][i]))

    def compaction(count):
        row, lane = iota((count * CAP, count * TILE), 0), iota((count * CAP, count * TILE), 1)
        block = (row * 2731) >> 16
        return [flag(lane == place) for place in places(block, row - block * CAP)]

    def expansion(count):
        row, lane = iota((count * TILE, count * CAP), 0), iota((count * TILE, count * CAP), 1)
        block = (lane * 2731) >> 16
        return [flag(row == place) for place in places(block, lane - block * CAP)]

    pack_parts = {count: compaction(count) for count in sorted(set(sizes))}
    spread_parts = {count: expansion(count) for count in sorted(set(sizes))}

    causal = iota((t, t), 0) >= iota((t, t), 1)
    for h in range(heads):
        head = pl.ds(h * 128, 128)
        scores = mm_nt(q[:, head], k[:, head])
        gap = jnp.where(causal, c_col[:, h : h + 1] - c_row[h : h + 1, :], 0.0)
        intra = jnp.where(causal, scores * jnp.exp(gap), 0.0).astype(BF16)
        r["within"][:, head] = mm(intra, v[:, head])

    wait(tr.at[pl.ds(0, n - 1)], m_r.at[0])
    wait(ur.at[pl.ds(0, n - 1)], m_r.at[1])

    def scan(b, state):
        sb[b] = state.astype(BF16)
        return jnp.exp(tr[b]) * state + ur[b].astype(F32)

    lax.fori_loop(0, n, scan, jnp.zeros((hd, 128), F32))
    seq_peers(lambda p: send(sb.at[p], se.at[s], m_s.at[2], m_r.at[2], (p, tp)))
    pending.append((se.at[pl.ds(0, n - 1)], m_s.at[2]))
    se[s] = sb[s]
    wait(se.at[pl.ds(0, n - 1)], m_r.at[2])

    attended = []
    for h in range(heads):
        head = pl.ds(h * 128, 128)
        state = se[h * per_head : (h + 1) * per_head].reshape(128, 128)
        head_out = r["within"][:, head] + mm(q[:, head], state) * jnp.exp(c_col[:, h : h + 1])
        mean = jnp.mean(head_out * head_out, axis=1, keepdims=True)
        attended.append((head_out * lax.rsqrt(mean + EPSILON)).astype(BF16))
    attention = jnp.concatenate(attended, axis=1)

    ps1, pr1, ps2, pr2 = (r[name] for name in ("ps1", "pr1", "ps2", "pr2"))
    for copy in weights[: tp_n + 1]:
        copy.wait()
    for to in (opposite, ahead, behind, y):
        ps1[to] = mm(attention, r["owv"][to * CORES + 1 - core]).astype(BF16)
        send(ps1.at[to], pr1.at[to], r["p1_s"].at[to], r["p1_r"].at[to], partner)
        pending.append((ps1.at[to], r["p1_s"].at[to]))

    def chip_sum(to):
        mine = mm(attention, r["owv"][to * CORES + core])
        wait(pr1.at[to], r["p1_r"].at[to])
        return mine + pr1[to].astype(F32)

    rl1 = r["rl1"]
    halves = (pl.ds(0, t // 2), pl.ds(t // 2, t // 2))
    ps2[2] = chip_sum(opposite).astype(BF16)
    for i, (_, device) in enumerate(sides):
        send(ps2.at[2, halves[i]], rl1.at[i], r["l1_s"].at[i], r["l1_r"].at[i], device)
        pending.append((rl1.at[i], r["l1_s"].at[i]))
    with_relay = []
    for i, (to, device) in enumerate(sides):
        mine = chip_sum(to)
        ps2[i, halves[1 - i]] = mine[(1 - i) * (t // 2) : (2 - i) * (t // 2)].astype(BF16)
        piece = (i, halves[1 - i])
        send(ps2.at[piece], pr2.at[piece], r["p3_s"].at[i], r["p3_r"].at[i], device)
        pending.append((ps2.at[piece], r["p3_s"].at[i]))
        with_relay.append(mine[i * (t // 2) : (i + 1) * (t // 2)])
    for i, (_, device) in enumerate(sides):
        wait(rl1.at[i], r["l1_r"].at[i])
        piece = (i, halves[i])
        ps2[piece] = (with_relay[i] + rl1[i].astype(F32)).astype(BF16)
        send(ps2.at[piece], pr2.at[piece], r["p2_s"].at[i], r["p2_r"].at[i], device)
        pending.append((ps2.at[piece], r["p2_s"].at[i]))
    hidden = res[...].astype(F32) + chip_sum(y)
    for i in range(2):
        wait(pr2.at[i, halves[1 - i]], r["p3_r"].at[i])
        wait(pr2.at[i, halves[i]], r["p2_r"].at[i])
        hidden = hidden + pr2[i].astype(F32)

    dsp, xr, ret = r["dsp"], r["xr"], r["ret"]
    scaled = (hidden * mult[...][None, :]).astype(BF16)
    to_pieces([r["pm"][i] for i in range(3)], scaled, dsp, pl.ds(0, n * TILE))

    def rows_of(index):
        return pl.ds(pl.multiple_of(index * TILE, TILE), TILE)

    home_group = [g for g, steps in enumerate(groups) if steps[0] == 0][0]
    home_slot = starts[home_group]

    def group_peers(g, sign, body):
        first = 0 if g != home_group else 1

        def step(i, carry):
            j = sizes[g] - 1 + first - i
            dz = groups[g][0]
            for chip in range(1, len(groups[g])):
                dz = jnp.where(j < chip * xs, dz, groups[g][chip])
            dx = lax.rem(j, xs)
            pz = lax.rem(z + zs + sign * dz, zs)
            px = lax.rem(x + xs + sign * dx, xs)
            body(starts[g] + j, pz * xs + px)
            return carry

        lax.fori_loop(first, sizes[g], step, 0)

    for g in range(len(groups)):
        group_peers(
            g,
            1,
            lambda j, p, g=g: send(
                dsp.at[:, rows_of(p)], xr.at[:, rows_of(j)], r["x_s"].at[g], r["x_r"].at[g], (p, tp)
            ),
        )
    def group_ref(g):
        skip = 1 if g == home_group else 0
        return xr.at[:, pl.ds((starts[g] + skip) * TILE, (sizes[g] - skip) * TILE)]

    for g in range(len(groups)):
        pending.append((group_ref(g), r["x_s"].at[g]))
    xr[:, home_slot * TILE : (home_slot + 1) * TILE] = dsp[:, rows_of(s)]

    sqs, sqr = r["sqs"], r["sqr"]
    high, low = split2(hidden * hidden)
    ones = jnp.ones((8, w), BF16)
    sqs[...] = (mm_nt(ones, high) + mm_nt(ones, low))[0:1]
    tp_peers(lambda p: send(sqs, sqr.at[tp], m_s.at[3], m_r.at[3], (s, p)))
    pending.append((sqr.at[pl.ds(0, tp_n - 1)], m_s.at[3]))
    sqr[tp] = sqs[...]
    partial_logits = mm_nt(scaled, r["rwv"][...])
    wait(sqr.at[pl.ds(0, tp_n - 1)], m_r.at[3])
    square_sum = sqr[0]
    for u in range(1, tp_n):
        square_sum = square_sum + sqr[u]
    inverse = to_column(lax.rsqrt(square_sum / (w * tp_n) + EPSILON))
    factors = jnp.zeros((n, 128), F32)
    lane = iota((t, 128), 1).astype(F32)
    for pick, slot in zip(picks, slots_c):
        chosen = flag(pick == names_lane)
        rest = jnp.where(slot == lane, inverse, 0.0)
        for _ in range(3):
            piece = rest.astype(BF16)
            rest = rest - piece.astype(F32)
            factors = factors + mm_tn(chosen, piece)
    fs, fr = r["fs"], r["fr"]
    for i in range(n):
        fs[i] = factors[i : i + 1]
    for g in range(len(groups)):
        group_peers(
            g,
            1,
            lambda j, p, g=g: send(
                fs.at[p], fr.at[j], m_s.at[6], m_r.at[6], (p, tp)
            ),
        )
    pending.append((fr.at[pl.ds(0, n - 1)], m_s.at[6]))
    fr[home_slot] = fs[s]

    cs, cr = r["cs"], r["cr"]
    logits = partial_logits * inverse
    for j in range(2):
        chosen = jnp.where(picks[j] == names_lane, logits, 0.0)
        cs[j] = to_row(jnp.sum(chosen, axis=1, keepdims=True))
    tp_peers(lambda p: send(cs, cr.at[tp], m_s.at[4], m_r.at[4], (s, p)))
    pending.append((cr.at[pl.ds(0, tp_n - 1)], m_s.at[4]))
    cr[tp] = cs[...]

    xg, mb, ps, pr = (r[name] for name in ("xg", "mb", "ps", "pr"))
    ys, yr, rl, hs = (r[name] for name in ("ys", "yr", "rl", "hs"))

    def slots_of(g, unit):
        return pl.ds(starts[g] * unit, sizes[g] * unit)

    def rows_in(g):
        return slots_of(g, CAP)

    def half_rows(g, i):
        return pl.ds(starts[g] * CAP + i * sizes[g] * CAP // 2, sizes[g] * CAP // 2)

    origins = (behind, ahead)

    def spread_out(g):
        wait(group_ref(g), r["x_r"].at[g])
        packed = from_pieces(pack_parts[sizes[g]], xr, slots_of(g, TILE)).astype(BF16)
        xg[tp, rows_in(g)] = packed
        piece = xg.at[tp, rows_in(g)]
        for i, (_, device) in enumerate(sides):
            send(piece, piece, r["a_s"].at[g, i], r["a_r"].at[g, i], device)
            pending.append((piece, r["a_s"].at[g, i]))
        if g in c["direct"]:
            across = (s, opposite * CORES + core)
            send(piece, piece, r["a_s"].at[g, 2], r["a_r"].at[g, 2], across)
            pending.append((piece, r["a_s"].at[g, 2]))
        send(piece, piece, r["b_s"].at[g, y], r["b_r"].at[g, y], partner)
        pending.append((piece, r["b_s"].at[g, y]))

    def pass_over(g, block):
        piece = xg.at[block * CORES + core, rows_in(g)]
        send(piece, piece, r["b_s"].at[g, block], r["b_r"].at[g, block], partner)
        pending.append((piece, r["b_s"].at[g, block]))

    def pass_on(g):
        for i, (_, device) in enumerate(sides):
            wait(xg.at[origins[i] * CORES + core, rows_in(g)], r["a_r"].at[g, i])
            if g not in c["direct"]:
                piece = xg.at[origins[i] * CORES + core, half_rows(g, i)]
                send(piece, piece, r["f_s"].at[g, i], r["f_r"].at[g, i], device)
                pending.append((piece, r["f_s"].at[g, i]))
            pass_over(g, origins[i])

    def pass_far(g):
        if g in c["direct"]:
            wait(xg.at[opposite * CORES + core, rows_in(g)], r["a_r"].at[g, 2])
        else:
            for i in range(2):
                wait(xg.at[opposite * CORES + core, half_rows(g, i)], r["f_r"].at[g, i])
        pass_over(g, opposite)

    waited = []

    def expert(g):
        for i in range(ys_n):
            wait(xg.at[i * CORES + 1 - core, rows_in(g)], r["b_r"].at[g, i])
        total = jnp.zeros((sizes[g] * CAP, c["f"]), F32)
        for i in range(ys_n):
            both = [xg[i * CORES + side, rows_in(g)] for side in range(CORES)]
            total = total + mm(jnp.concatenate(both, axis=1), r["upv"][i])
        if not waited:
            wait(fr.at[pl.ds(0, n - 1)], m_r.at[6])
            waited.append(g)
        mine = range(starts[g], starts[g] + sizes[g])
        spots = [jnp.broadcast_to(fr[j], (CAP, 128)) for j in mine]
        spots = jnp.concatenate(spots, axis=0)
        spot_row, spot_lane = iota((sizes[g] * CAP, 128), 0), iota((sizes[g] * CAP, 128), 1)
        spot_row = spot_row - ((spot_row * 2731) >> 16) * CAP
        total = total * jnp.sum(jnp.where(spot_lane == spot_row, spots, 0.0), axis=1, keepdims=True)
        hidden_rows = (total / (1.0 + jnp.exp(-total))).astype(BF16)
        for i in range(ys_n):
            part = mm(hidden_rows, r["dnv"][i])
            left, right = part[:, :w], part[:, w:]
            mb[i, rows_in(g)] = jnp.where(core == 0, left, right)
            ps[i, rows_in(g)] = jnp.where(core == 0, right, left).astype(BF16)
            piece = (i, rows_in(g))
            send(ps.at[piece], pr.at[piece], r["c_s"].at[g, i], r["c_r"].at[g, i], partner)
            pending.append((ps.at[piece], r["c_s"].at[g, i]))

    def chip_rows(g, to, part):
        return mb[to, part] + pr[to, part].astype(F32)

    def sum_far(g):
        for i in range(ys_n):
            wait(pr.at[i, rows_in(g)], r["c_r"].at[g, i])
        for i, (_, device) in enumerate(sides):
            part = half_rows(g, i)
            ys[2, part] = chip_rows(g, opposite, part).astype(BF16)
            send(ys.at[2, part], rl.at[part], r["l_s"].at[g, i], r["l_r"].at[g, i], device)
            pending.append((ys.at[2, part], r["l_s"].at[g, i]))
        for i, (to, device) in enumerate(sides):
            part = half_rows(g, 1 - i)
            ys[i, part] = chip_rows(g, to, part).astype(BF16)
            send(ys.at[i, part], yr.at[i, part], r["e_s"].at[g, i], r["e_r"].at[g, i], device)
            pending.append((ys.at[i, part], r["e_s"].at[g, i]))

    def sum_near(g):
        for i, (to, device) in enumerate(sides):
            part = half_rows(g, i)
            wait(rl.at[part], r["l_r"].at[g, i])
            ys[i, part] = (chip_rows(g, to, part) + rl[part].astype(F32)).astype(BF16)
            send(ys.at[i, part], yr.at[i, part], r["d_s"].at[g, i], r["d_r"].at[g, i], device)
            pending.append((ys.at[i, part], r["d_s"].at[g, i]))

    def home(g):
        total = chip_rows(g, y, rows_in(g))
        for i in range(2):
            wait(yr.at[i, half_rows(g, 1 - i)], r["e_r"].at[g, i])
            wait(yr.at[i, half_rows(g, i)], r["d_r"].at[g, i])
            total = total + yr[i, rows_in(g)].astype(F32)
        to_pieces(spread_parts[sizes[g]], total.astype(BF16), hs, slots_of(g, TILE))
        group_peers(
            g,
            -1,
            lambda j, p: send(
                hs.at[:, rows_of(j)], ret.at[:, rows_of(s)], r["h_s"].at[g], m_r.at[5], (p, tp)
            ),
        )
        last_sent.append((group_ref(g), r["h_s"].at[g]))
        if g == home_group:
            ret[:, rows_of(s)] = hs[:, home_slot * TILE : (home_slot + 1) * TILE]

    for copy in weights[tp_n + 1 :]:
        copy.wait()
    stages = (spread_out, pass_on, pass_far, expert, sum_far, sum_near, home)
    todo = {g: list(stages) for g in range(len(groups))}
    for g in c["order"]:
        todo[g].pop(0)(g)

    wait(cr.at[pl.ds(0, tp_n - 1)], m_r.at[4])
    gates = []
    for j in range(2):
        logit = cr[0, j]
        for u in range(1, tp_n):
            logit = logit + cr[u, j]
        gates.append(jax.nn.sigmoid(logit))
    both = gates[0] + gates[1]
    shares = [to_column(gate / both) for gate in gates]
    for ref, sem in pending:
        wait(ref, sem)
    wait(ret.at[:, pl.ds(0, (n - 1) * TILE)], m_r.at[5])
    mixed = hidden
    for j in range(2):
        parts = [r["q"][j, i] for i in range(3)]
        mixed = mixed + shares[j] * from_pieces(parts, ret, pl.ds(0, n * TILE))
    out[...] = mixed.astype(BF16)

    for ref, sem in last_sent:
        wait(ref, sem)


DIRECT = {8: ()}
GROUPS = {8: [(1, 7), (2, 6), (3, 5), (0, 4)]}
ORDERS = {8: [0, 1, 0, 2, 0, 1, 3, 0, 2, 1, 0, 1, 3, 1, 2, 2, 0, 2, 3, 3, 1, 2, 0, 3, 1, 2, 3, 3]}


def stepped(count, stages=7):
    return [
        step - lag
        for step in range(count + stages - 1)
        for lag in range(stages)
        if 0 <= step - lag < count
    ]


def body(
    sizes,
    queries,
    keys,
    values,
    log_decay,
    residual,
    out_weight,
    prenorm_multiplier,
    router_weight,
    picked_unit_indices,
    expert_up_weight,
    down_weight,
):
    n, xs, zs, ys = sizes
    half = zs // 2
    groups = GROUPS.get(zs) or [(d, zs - d) for d in range(1, half)] + [(0, half)]
    order = ORDERS.get(zs) or stepped(len(groups))
    heads = log_decay.shape[0]
    c = dict(
        n=n,
        x=xs,
        z=zs,
        y=ys,
        groups=groups,
        order=order,
        direct=DIRECT.get(zs, ()),
        g=len(groups),
        heads=heads,
        t=queries.shape[0],
        a=queries.shape[1],
        w=residual.shape[1],
        f=expert_up_weight.shape[2],
        hd=heads * 128 // n,
    )
    scratch = scratch_of(c)
    vmem, anywhere = pl.BlockSpec(memory_space=pltpu.VMEM), pl.BlockSpec(memory_space=pl.ANY)
    return pl.pallas_call(
        functools.partial(kernel, c, list(scratch)),
        out_shape=jax.ShapeDtypeStruct(residual.shape, BF16),
        in_specs=[vmem] * 7 + [anywhere] * 4,
        out_specs=vmem,
        scratch_shapes=list(scratch.values()),
        compiler_params=pltpu.CompilerParams(
            collective_id=0, has_side_effects=True, vmem_limit_bytes=56 * 1024 * 1024
        ),
    )(
        queries,
        keys,
        values,
        log_decay,
        residual,
        prenorm_multiplier,
        picked_unit_indices.T,
        out_weight,
        router_weight.T,
        expert_up_weight,
        down_weight,
    )


def solution(mesh):
    n = mesh.shape["seq"]
    xs = 4 if n % 4 == 0 and n > 4 else 2
    sizes = (n, xs, n // xs, mesh.shape["tp"] // CORES)
    in_specs = (
        P("seq", "tp"),
        P("seq", "tp"),
        P("seq", "tp"),
        P("tp", "seq"),
        P("seq", "tp"),
        P("tp", None),
        P("tp"),
        P(),
        P("seq", None),
        P("seq", None, "tp"),
        P("seq", "tp", None),
    )
    return jax.shard_map(
        functools.partial(body, sizes),
        mesh=mesh,
        in_specs=in_specs,
        out_specs=P("seq", "tp"),
        check_vma=False,
    )
```
